32 devices in a mesh: cam: 2 (over x), band: 4 (over z), obj: 4 (over y, core).
Axes of the slice: x: 2, y: 2, z: 4, core: 2. Of those that a mesh axis runs over, the one named last changes fastest.
Arguments:
- queries: bfloat16 [4, 6, 4, 128, 1280], P('obj', 'cam', 'band'), may hold values from -6 to 6
- keys: bfloat16 [4, 6, 4, 128, 1280], P('obj', 'cam', 'band'), may hold values from -6 to 6
- values: bfloat16 [4, 6, 4, 128, 1280], P('obj', 'cam', 'band'), may hold values from -6 to 6
- d_out: bfloat16 [4, 6, 4, 128, 2432], P('obj', 'cam', 'band'), may hold values from -6 to 6
- w_out: bfloat16 [1280, 2432], P(('band', 'obj'), 'cam'), may hold values from -0.15625 to 0.15625
Outputs:
- grad_q: bfloat16 [4, 6, 4, 128, 1280], P('obj', 'cam', 'band')
- grad_k: bfloat16 [4, 6, 4, 128, 1280], P('obj', 'cam', 'band')
- grad_v: bfloat16 [4, 6, 4, 128, 1280], P('obj', 'cam', 'band')
- grad_wo: float32 [1280, 2432], P(('band', 'obj'), 'cam')
The draws below stay inside these ranges and needn't reach their ends.
All inputs are finite; a program needn't handle non-finite values.
Results may differ from the reference program's by a relative error of at most 0.0095.
Values may be sent and summed in bfloat16 or wider, within the bound.
No kernel may reach another device: no remote copies, remote signals or barrier semaphores. Data moves between devices by JAX's collectives and lax.ppermute only.
A program may use at most 128 MiB of HBM per device.

```python
import jax
import jax.numpy as jnp
from jax import lax

D = 2432
HEADS = 20
HEAD_DIM = 64
VIEWS = 6
COLS = 128
HD = 1280
ROWS = 4
OBJS = 4
TOKENS = 12288


def draw_queries(key, part):
    shape = (OBJS, VIEWS, ROWS, COLS, HD)
    values = jnp.clip(jax.random.normal(jax.random.fold_in(key, 1), shape, jnp.float32), -6.0, 6.0)
    return values.astype(jnp.bfloat16)


def draw_keys(key, part):
    shape = (OBJS, VIEWS, ROWS, COLS, HD)
    values = jnp.clip(jax.random.normal(jax.random.fold_in(key, 2), shape, jnp.float32), -6.0, 6.0)
    return values.astype(jnp.bfloat16)


def block_scale(rng, extent, cuts, smallest, largest):
    gain = 1.0
    for dim, blocks in cuts:
        draws = jax.random.uniform(jax.random.fold_in(jax.random.fold_in(rng, 6), dim), (blocks,), jnp.float32, smallest / len(cuts), largest / len(cuts))
        gain = gain * jnp.repeat(jnp.exp(draws), extent[dim] // blocks).reshape((-1,) + (1,) * (len(extent) - 1 - dim))
    return gain


def noise(key, extent, spread, reach, pieces=(), dtype=jnp.bfloat16):
    values = jax.random.normal(key, extent, jnp.float32) * spread
    if len(pieces) > 0:
        values = block_scale(key, extent, pieces, -0.22, 0.18) * values
    return jnp.clip(values, min=-reach, max=reach).astype(dtype)


def setup_inputs(seed: int = 0) -> dict:
    key_of = jax.random.split(jax.random.key(seed), 6)
    queries = draw_queries(jax.random.fold_in(key_of[5], 71), 0)
    keys = draw_keys(jax.random.fold_in(key_of[5], 71), 0)
    values = noise(key_of[2], (OBJS, VIEWS, ROWS, COLS, HD), 1.0, 6.0, ((0, 4), (1, 2), (2, 4)))
    d_out = noise(key_of[3], (OBJS, VIEWS, ROWS, COLS, D), 1.0, 6.0, ((0, 4), (1, 2), (2, 4)))
    w_out = noise(key_of[4], (HD, D), HD ** -0.5, 0.15625, ((0, 16), (1, 2)))
    return {"queries": queries, "keys": keys, "values": values, "d_out": d_out, "w_out": w_out}


def rounded(x):
    return lax.optimization_barrier(x.astype(jnp.bfloat16)).astype(jnp.float32)


def group_backward(parts):
    q_group, k_group, v_group, d_group = parts
    qf = q_group.astype(jnp.float32)
    kf = k_group.astype(jnp.float32)
    vf = v_group.astype(jnp.float32)
    df = d_group.astype(jnp.float32)
    scores = jnp.einsum("qhe,khe->hqk", qf, kf) * 0.125
    top = jnp.max(scores, axis=-1, keepdims=True)
    expd = jnp.exp(scores - top)
    probs = expd / jnp.sum(expd, axis=-1, keepdims=True)
    probs_b = rounded(probs)
    att = jnp.einsum("hqk,khe->qhe", probs_b, vf).astype(jnp.bfloat16)
    d_probs = jnp.einsum("qhe,khe->hqk", df, vf)
    delta = jnp.sum(probs * d_probs, axis=-1, keepdims=True)
    d_scores_b = rounded(probs * (d_probs - delta))
    grad_q = (jnp.einsum("hqk,khe->qhe", d_scores_b, kf) * 0.125).astype(jnp.bfloat16)
    grad_k = (jnp.einsum("hqk,qhe->khe", d_scores_b, qf) * 0.125).astype(jnp.bfloat16)
    grad_v = jnp.einsum("hqk,qhe->khe", probs_b, df).astype(jnp.bfloat16)
    return grad_q, grad_k, grad_v, att


def to_groups(x):
    return x.transpose(0, 2, 1, 3, 4).reshape(OBJS * ROWS, VIEWS * COLS, HEADS, HEAD_DIM)


def from_groups(x):
    return x.reshape(OBJS, ROWS, VIEWS, COLS, HD).transpose(0, 2, 1, 3, 4)


def reference(queries, keys, values, d_out, w_out):
    flat_out = d_out.reshape(TOKENS, D)
    d_att = jnp.dot(flat_out, w_out.T, preferred_element_type=jnp.float32).astype(jnp.bfloat16)
    d_att = d_att.reshape(OBJS, VIEWS, ROWS, COLS, HD)
    results = lax.map(group_backward, (to_groups(queries), to_groups(keys), to_groups(values), to_groups(d_att)))
    grad_q, grad_k, grad_v, att = [from_groups(r) for r in results]
    flat_att = att.reshape(TOKENS, HD)
    grad_wo = jnp.dot(flat_att.T, flat_out, preferred_element_type=jnp.float32)
    grad_wo = grad_wo * (jnp.float32(TOKENS) ** -0.5)
    return grad_q, grad_k, grad_v, grad_wo
```

```python
import jax
import jax.numpy as jnp
from jax import lax
from jax.experimental import pallas as pl
from jax.experimental.pallas import tpu as pltpu
from jax.sharding import PartitionSpec as P

BF16, F32 = jnp.bfloat16, jnp.float32
HEAD = 64
PAIR = 2 * HEAD
SCALE = HEAD**-0.5
LOG2E = 1.4426950408889634
NT = (((1,), (1,)), ((), ()))
PARAMS = pltpu.CompilerParams(vmem_limit_bytes=48 * 2**20)


def mm(a, b):
    return jnp.dot(a, b, preferred_element_type=F32)


def nt(a, b):
    return lax.dot_general(a, b, NT, preferred_element_type=F32)


def stack_heads(x):
    lane = lax.broadcasted_iota(jnp.int32, x.shape, 1)
    zero = jnp.zeros_like(x)
    return jnp.concatenate([jnp.where(lane < HEAD, x, zero), jnp.where(lane < HEAD, zero, x)], 0)


def spread_heads(x):
    zero = jnp.zeros((HEAD, x.shape[1]), x.dtype)
    return jnp.concatenate(
        [jnp.concatenate([x[:HEAD], zero], 0), jnp.concatenate([zero, x[HEAD:]], 0)], 1
    )


def own_heads(x):
    n = x.shape[1] // 2
    return jnp.concatenate([x[:HEAD, :n], x[HEAD:, n:]], 0)


def pack_kernel(k_ref, v_ref, out_ref):
    n = k_ref.shape[0]
    out_ref[:n] = k_ref[...]
    out_ref[n:] = v_ref[...]


def pack(k, v, first, pairs):
    n = k.shape[0]
    return pl.pallas_call(
        pack_kernel,
        grid=(pairs,),
        in_specs=[pl.BlockSpec((n, PAIR), lambda i: (0, first + i))] * 2,
        out_specs=pl.BlockSpec((2 * n, PAIR), lambda i: (0, i)),
        out_shape=jax.ShapeDtypeStruct((2 * n, pairs * PAIR), BF16),
        compiler_params=PARAMS,
        name="pack",
    )(k, v)


def attend_kernel(q_ref, k_ref, v_ref, kv_ref, *refs):
    p_ref, att_ref = refs[-2:]
    n = q_ref.shape[0]
    k = jnp.concatenate([k_ref[...], kv_ref[:n]], 0)
    v = jnp.concatenate([v_ref[...], kv_ref[n:]], 0)
    s = nt(k, stack_heads(q_ref[...]))
    top = jnp.max(s, axis=0, keepdims=True)
    e = jnp.exp2((s - top) * (SCALE * LOG2E))
    p = e * (1.0 / jnp.sum(e, axis=0, keepdims=True))
    p_ref[0] = p
    att_ref[...] = own_heads(mm(v.T, p.astype(BF16))).astype(BF16)


def attend(q, k, v, kv, att, first, pairs):
    n, width = q.shape
    ins = [q, k, v, kv] + ([] if att is None else [att])
    specs = [pl.BlockSpec((n, PAIR), lambda i: (0, first + i))] * 3
    specs += [pl.BlockSpec((2 * n, PAIR), lambda i: (0, i))]
    specs += [pl.BlockSpec(memory_space=pl.ANY)] * (len(ins) - 4)
    return pl.pallas_call(
        attend_kernel,
        grid=(pairs,),
        in_specs=specs,
        out_specs=[
            pl.BlockSpec((1, 2 * n, 2 * n), lambda i: (i, 0, 0)),
            pl.BlockSpec((PAIR, n), lambda i: (first + i, 0)),
        ],
        out_shape=[
            jax.ShapeDtypeStruct((pairs, 2 * n, 2 * n), F32),
            jax.ShapeDtypeStruct((width, n), BF16),
        ],
        input_output_aliases={} if att is None else {4: 1},
        compiler_params=PARAMS,
        name="attend",
    )(*ins)


def back_kernel(p_ref, q_ref, k_ref, v_ref, kv_ref, d_ref, *refs):
    dq_ref, dk_ref, dv_ref, far_ref = refs[-4:]
    n = q_ref.shape[0]
    k = jnp.concatenate([k_ref[...], kv_ref[:n]], 0)
    v = jnp.concatenate([v_ref[...], kv_ref[n:]], 0)
    q = stack_heads(q_ref[...])
    d = spread_heads(d_ref[...])
    p = p_ref[0]
    dp = mm(v, d)
    delta = jnp.sum(p * dp, axis=0, keepdims=True)
    ds = (p * (dp - delta)).astype(BF16)
    dv = nt(p.astype(BF16), d)
    dk = mm(ds, q) * SCALE
    dq = own_heads(mm(k.T, ds)) * SCALE
    dq_ref[...] = dq.T.astype(BF16)
    dk_ref[...] = dk[:n]
    dv_ref[...] = dv[:n]
    far_ref[:n] = dk[n:].astype(BF16)
    far_ref[n:] = dv[n:].astype(BF16)


def back(p, q, k, v, kv, d, dq, first, pairs):
    n, width = q.shape
    ins = [p, q, k, v, kv, d] + ([] if dq is None else [dq])
    col = pl.BlockSpec((n, PAIR), lambda i: (0, first + i))
    own = pl.BlockSpec((n, PAIR), lambda i: (0, i))
    both = pl.BlockSpec((2 * n, PAIR), lambda i: (0, i))
    specs = [pl.BlockSpec((1, 2 * n, 2 * n), lambda i: (i, 0, 0)), col, col, col, both]
    specs += [pl.BlockSpec((PAIR, n), lambda i: (first + i, 0))]
    specs += [pl.BlockSpec(memory_space=pl.ANY)] * (len(ins) - 6)
    return pl.pallas_call(
        back_kernel,
        grid=(pairs,),
        in_specs=specs,
        out_specs=[col, own, own, both],
        out_shape=[
            jax.ShapeDtypeStruct((n, width), BF16),
            jax.ShapeDtypeStruct((n, pairs * PAIR), F32),
            jax.ShapeDtypeStruct((n, pairs * PAIR), F32),
            jax.ShapeDtypeStruct((2 * n, pairs * PAIR), BF16),
        ],
        input_output_aliases={} if dq is None else {6: 0},
        compiler_params=PARAMS,
        name="back",
    )(*ins)


def finish_kernel(dk_ref, dv_ref, far_ref, *refs):
    gk_ref, gv_ref = refs[-2:]
    n = dk_ref.shape[0]
    gk_ref[...] = (dk_ref[...] + far_ref[:n].astype(F32)).astype(BF16)
    gv_ref[...] = (dv_ref[...] + far_ref[n:].astype(F32)).astype(BF16)


def finish(dk, dv, far, grads, first, pairs, width):
    n = dk.shape[0]
    own = pl.BlockSpec((n, PAIR), lambda i: (0, i))
    specs = [own, own, pl.BlockSpec((2 * n, PAIR), lambda i: (0, i))]
    specs += [pl.BlockSpec(memory_space=pl.ANY)] * len(grads)
    return pl.pallas_call(
        finish_kernel,
        grid=(pairs,),
        in_specs=specs,
        out_specs=[pl.BlockSpec((n, PAIR), lambda i: (0, first + i))] * 2,
        out_shape=[jax.ShapeDtypeStruct((n, width), BF16)] * 2,
        input_output_aliases={3: 0, 4: 1} if grads else {},
        compiler_params=PARAMS,
        name="finish",
    )(dk, dv, far, *grads)


def project_kernel(slot_ref, w0, w1, w2, w3, own_ref, other_ref, out_own, out_other):
    rows = w0.shape[0]
    w = jnp.concatenate([w0[...], w1[...], w2[...], w3[...]], 0)
    for d_ref, out_ref in ((own_ref, out_own), (other_ref, out_other)):
        res = nt(w, d_ref[...]).astype(BF16)
        for j in range(4):
            out_ref[slot_ref[j]] = res[j * rows : (j + 1) * rows]


def project(slots, blocks, own, other):
    rows, depth = blocks[0].shape
    n = own.shape[0]
    whole = pl.BlockSpec(memory_space=pltpu.VMEM)
    return pl.pallas_call(
        project_kernel,
        in_specs=[pl.BlockSpec(memory_space=pltpu.SMEM)] + [whole] * 6,
        out_specs=[whole] * 2,
        out_shape=[jax.ShapeDtypeStruct((4, rows, n), BF16)] * 2,
        compiler_params=PARAMS,
        name="project",
    )(slots, *blocks, own, other)


def outer_kernel(slot_ref, a_own, a_other, d_own, d_other, o0, o1, o2, o3):
    rows = a_own.shape[1]
    left = [
        jnp.concatenate([ref[slot_ref[j]] for j in range(4)], 0) for ref in (a_own, a_other)
    ]
    res = (mm(left[0], d_own[...]) + mm(left[1], d_other[...])).astype(BF16)
    for j, ref in enumerate((o0, o1, o2, o3)):
        ref[...] = res[j * rows : (j + 1) * rows]


def outer(slots, a_own, a_other, d_own, d_other):
    rows, depth = a_own.shape[1], d_own.shape[1]
    whole = pl.BlockSpec(memory_space=pltpu.VMEM)
    return pl.pallas_call(
        outer_kernel,
        in_specs=[pl.BlockSpec(memory_space=pltpu.SMEM)] + [whole] * 4,
        out_specs=[whole] * 4,
        out_shape=[jax.ShapeDtypeStruct((rows, depth), BF16)] * 4,
        compiler_params=PARAMS,
        name="outer",
    )(slots, a_own, a_other, d_own, d_other)


def swap(x, axis, bit=1):
    size = lax.axis_size(axis)
    return lax.ppermute(x, axis, [(i, i ^ bit) for i in range(size)])


def shift(x, axis, step):
    size = lax.axis_size(axis)
    return lax.ppermute(x, axis, [(i, (i + step) % size) for i in range(size)])


def ordered(mine, theirs, flag, axis):
    return jnp.where(
        flag == 0,
        jnp.concatenate([mine, theirs], axis),
        jnp.concatenate([theirs, mine], axis),
    )


ORDER = (2, 1, 3, 0)


def body(queries, keys, values, d_out, w_out):
    shape = queries.shape
    width, model_width = shape[4], d_out.shape[4]
    n = shape[0] * shape[1] * shape[2] * shape[3]
    q, k, v = (x.reshape(n, width) for x in (queries, keys, values))
    flat = d_out.reshape(n, model_width)
    cams, bands, objs = (lax.axis_size(a) for a in ("cam", "band", "obj"))
    total = n * cams * bands * objs
    cam, band, obj = (lax.axis_index(a) for a in ("cam", "band", "obj"))
    core, line = obj % 2, obj // 2
    blocked = bands == 4 and objs == 4
    pairs = width // PAIR
    chunks = [(i, min(2, pairs - i)) for i in range(0, pairs, 2)]

    w_cols = ordered(w_out, swap(w_out, "cam"), cam, 1)
    sent = [swap(pack(k, v, first, count), "cam") for first, count in chunks]
    if blocked:
        flat_other = swap(flat, "obj")
        held = [shift(w_cols, "band", s) for s in ORDER[:3]] + [w_cols]
        passed = [swap(w, "obj", 2) for w in held]
        into = jnp.stack([(band - s) % 4 for s in ORDER]).astype(jnp.int32)

    att, probs = None, []
    for (first, count), kv in zip(chunks, sent):
        p, att = attend(q, k, v, kv, att, first, count)
        probs.append(p)

    if blocked:
        mine_o, mine_x = project(into, held, flat, flat_other)
        far_o, far_x = project(into, passed, flat, flat_other)
        got = swap(jnp.stack([mine_x, far_x], 1), "obj")
        got = got.reshape(4, 2, 1, -1, n)
        both = jnp.stack([mine_o, far_o], 1).reshape(4, 2, 1, -1, n)
        both = ordered(both, got, core, 2)
        both = jnp.where(line == 0, both, both[:, ::-1])
        d_att = both.reshape(width, n)
    else:
        full = lax.all_gather(w_cols, ("band", "obj"), axis=0, tiled=True)
        d_att = nt(full, flat).astype(BF16)

    dq, parts = None, []
    for (first, count), kv, p in zip(chunks, sent, probs):
        dq, dk, dv, far = back(p, q, k, v, kv, d_att, dq, first, count)
        parts.append((dk, dv, swap(far, "cam")))

    if blocked:
        rows = w_out.shape[0]
        blocks = att.reshape(bands * 2, 2, rows, n)
        a_own = lax.dynamic_index_in_dim(blocks, core, 1, keepdims=False)
        a_other = swap(lax.dynamic_index_in_dim(blocks, 1 - core, 1, keepdims=False), "obj")
        out_of = jnp.stack([(band + s) % 4 for s in ORDER]).astype(jnp.int32) * 2
        away = outer(out_of + 1 - line, a_own, a_other, flat, flat_other)
        stay = outer(out_of + line, a_own, a_other, flat, flat_other)
        sums = [a.astype(F32) + swap(b, "obj", 2).astype(F32) for a, b in zip(stay, away)]
        total_rows = sums[3]
        for s, x in zip(ORDER[:3], sums):
            total_rows = total_rows + shift(x.astype(BF16), "band", s).astype(F32)
    else:
        total_rows = lax.psum_scatter(mm(att, flat), ("band", "obj"), scatter_dimension=0, tiled=True)
    half = w_out.shape[1]
    left, right = total_rows[:, :half], total_rows[:, half:]
    mine = jnp.where(cam == 0, left, right)
    theirs = jnp.where(cam == 0, right, left).astype(BF16)
    grad_wo = (mine + swap(theirs, "cam").astype(F32)) * float(total) ** (-0.5)

    grads = []
    for (first, count), (dk, dv, far) in zip(chunks, parts):
        grads = finish(dk, dv, far, grads, first, count, width)
    return (dq.reshape(shape), grads[0].reshape(shape), grads[1].reshape(shape), grad_wo)


def solution(mesh):
    token = P("obj", "cam", "band", None, None)
    weight = P(("band", "obj"), "cam")
    return jax.shard_map(
        body,
        mesh=mesh,
        in_specs=(token, token, token, token, weight),
        out_specs=(token, token, token, weight),
        check_vma=False,
    )
```

```python
import jax
import jax.numpy as jnp
from jax import lax
from jax.experimental import pallas as pl
from jax.experimental.pallas import tpu as pltpu
from jax.sharding import PartitionSpec as P

BF16, F32 = jnp.bfloat16, jnp.float32
HEAD = 64
PAIR = 2 * HEAD
SCALE = HEAD**-0.5
LOG2E = 1.4426950408889634
NT = (((1,), (1,)), ((), ()))
ANY = pl.BlockSpec(memory_space=pl.ANY)
VMEM = pl.BlockSpec(memory_space=pltpu.VMEM)
SMEM = pl.BlockSpec(memory_space=pltpu.SMEM)
TOKEN = (8, 128)
BIG = 60
FLOPS_PER_US = 1150e6 * 0.5
CHUNKS = (4, 4, 2)
PARTS = 2


def mm(a, b):
    return jnp.dot(a, b, preferred_element_type=F32)


def nt(a, b):
    return lax.dot_general(a, b, NT, preferred_element_type=F32)


def run(kernel, name, ins, in_specs, outs, out_specs, grid=(), after=(), alias=(), scratch=(), us=1, vmem=24, slots=None):
    hold = [*alias, *after]
    n_slots, n_in, n_hold, n_out = int(slots is not None), len(ins), len(hold), len(outs)

    def wrapped(*refs):
        last = n_slots + n_in + n_hold + n_out
        kernel(*refs[: n_slots + n_in], *refs[last - n_out : last], *refs[last + 1 :])
        refs[last][...] = jnp.zeros(TOKEN, F32)

    token_spec = pl.BlockSpec(TOKEN, lambda *_: (0, 0)) if grid else VMEM
    *results, token = pl.pallas_call(
        wrapped,
        grid_spec=pltpu.PrefetchScalarGridSpec(
            num_scalar_prefetch=n_slots,
            grid=grid,
            in_specs=[*in_specs, *[ANY] * n_hold],
            out_specs=[*out_specs, token_spec],
            scratch_shapes=list(scratch),
        ),
        out_shape=[*[jax.ShapeDtypeStruct(s, t) for s, t in outs], jax.ShapeDtypeStruct(TOKEN, F32)],
        input_output_aliases={n_slots + n_in + i: i for i in range(len(alias))},
        compiler_params=pltpu.CompilerParams(vmem_limit_bytes=vmem * 2**20),
        cost_estimate=pl.CostEstimate(flops=int(us * FLOPS_PER_US), transcendentals=0, bytes_accessed=0),
        name=name,
    )(*([] if slots is None else [slots]), *ins, *hold)
    return results, token


def whole(x):
    shape = x if isinstance(x, tuple) else x.shape
    return pl.BlockSpec(shape, lambda *_: (0,) * len(shape))


def stack_heads(x):
    lane = lax.broadcasted_iota(jnp.int32, x.shape, 1)
    zero = jnp.zeros_like(x)
    return jnp.concatenate([jnp.where(lane < HEAD, x, zero), jnp.where(lane < HEAD, zero, x)], 0)


def spread_heads(x):
    zero = jnp.zeros((HEAD, x.shape[1]), x.dtype)
    return jnp.concatenate(
        [jnp.concatenate([x[:HEAD], zero], 0), jnp.concatenate([zero, x[HEAD:]], 0)], 1
    )


def own_heads(x):
    n = x.shape[1] // 2
    return jnp.concatenate([x[:HEAD, :n], x[HEAD:, n:]], 0)


def column(n, first):
    return pl.BlockSpec((n, PAIR), lambda i: (0, first + i))


def pack_kernel(k_ref, v_ref, out_ref):
    n = k_ref.shape[0]
    out_ref[:n] = k_ref[...]
    out_ref[n:] = v_ref[...]


def pack(k, v, first, pairs, after):
    n = k.shape[0]
    (out,), token = run(
        pack_kernel, "pack", [k, v], [column(n, first)] * 2,
        [((2 * n, pairs * PAIR), BF16)], [column(2 * n, 0)], (pairs,), after, us=pairs * 0.4,
    )
    return out, token


def attend_kernel(q_ref, k_ref, v_ref, kv_ref, att_ref, p_ref, stat_ref, far_ref):
    n = q_ref.shape[0]
    k = jnp.concatenate([k_ref[...], kv_ref[:n]], 0)
    v = jnp.concatenate([v_ref[...], kv_ref[n:]], 0)
    s = nt(k, stack_heads(q_ref[...]))
    top = jnp.max(s, axis=0, keepdims=True)
    e = jnp.exp2((s - top) * (SCALE * LOG2E))
    p_ref[0] = e
    inverse = 1.0 / jnp.sum(e, axis=0, keepdims=True)
    stat_ref[0] = jnp.concatenate([top, inverse], 0)
    att_ref[...] = own_heads(mm(v.T, e.astype(BF16)) * inverse).astype(BF16)
    far_ref[...] = kv_ref[...]


def attend(q, k, v, kv, state, first, pairs, after):
    n, width = q.shape
    count = width // PAIR
    at = lambda *block: pl.BlockSpec((1, *block), lambda i: (first + i, 0, 0))
    return run(
        attend_kernel, "attend",
        [q, k, v, kv], [column(n, first)] * 3 + [column(2 * n, 0)],
        [
            ((width, n), BF16), ((count, 2 * n, 2 * n), F32),
            ((count, 2, 2 * n), F32), ((2 * n, width), BF16),
        ],
        [pl.BlockSpec((PAIR, n), lambda i: (first + i, 0)), at(2 * n, 2 * n), at(2, 2 * n), column(2 * n, first)],
        (pairs,), after, state, us=1.9 * pairs, vmem=BIG,
    )


def back_kernel(p_ref, stat_ref, q_ref, k_ref, v_ref, kv_ref, d_ref, dq_ref, dk_ref, dv_ref, out_ref):
    n = q_ref.shape[0]
    k = jnp.concatenate([k_ref[...], kv_ref[:n]], 0)
    v = jnp.concatenate([v_ref[...], kv_ref[n:]], 0)
    q = stack_heads(q_ref[...])
    d = spread_heads(d_ref[...])
    p = p_ref[0] * stat_ref[0, 1:]
    dp = mm(v, d)
    delta = jnp.sum(p * dp, axis=0, keepdims=True)
    ds = (p * (dp - delta)).astype(BF16)
    dv_ref[...] = nt(p[:n].astype(BF16), d)
    dk_ref[...] = mm(ds[:n], q)
    dq_ref[...] = (own_heads(mm(k.T, ds)) * SCALE).T.astype(BF16)
    out_ref[0] = jnp.concatenate([stat_ref[0], delta], 0)


def back(state, q, k, v, d, done, first, pairs, after):
    n, width = q.shape
    _, p, stat, kv = state
    at = lambda *block: pl.BlockSpec((1, *block), lambda i: (first + i, 0, 0))
    return run(
        back_kernel, "back",
        [p, stat, q, k, v, kv, d],
        [at(2 * n, 2 * n), at(2, 2 * n)]
        + [column(n, first)] * 3
        + [column(2 * n, first), pl.BlockSpec((PAIR, n), lambda i: (first + i, 0))],
        [((n, width), BF16)] + [((n, width), F32)] * 2 + [((width // PAIR, 3, 2 * n), F32)],
        [column(n, first)] * 3 + [at(3, 2 * n)],
        (pairs,), after, done, us=2 * pairs, vmem=BIG,
    )


def cross_kernel(q_ref, k_ref, v_ref, d_ref, stat_ref, dk_ref, dv_ref, gk_ref, gv_ref):
    q = stack_heads(q_ref[...])
    d = spread_heads(d_ref[...])
    top, inverse, delta = (stat_ref[0, i : i + 1] for i in range(3))
    p = jnp.exp2((nt(k_ref[...], q) - top) * (SCALE * LOG2E)) * inverse
    ds = (p * (mm(v_ref[...], d) - delta)).astype(BF16)
    gv_ref[...] = (nt(p.astype(BF16), d) + dv_ref[...]).astype(BF16)
    gk_ref[...] = ((mm(ds, q) + dk_ref[...]) * SCALE).astype(BF16)


def cross(q, k, v, d, share, after):
    n, width = q.shape
    pairs = width // PAIR
    dk, dv, stat = share
    return run(
        cross_kernel, "cross",
        [q, k, v, d, stat, dk, dv],
        [column(n, 0)] * 3
        + [pl.BlockSpec((PAIR, n), lambda i: (i, 0)), pl.BlockSpec((1, 3, 2 * n), lambda i: (i, 0, 0))]
        + [column(n, 0)] * 2,
        [((n, width), BF16)] * 2, [column(n, 0)] * 2, (pairs,), after, us=1.5 * pairs,
    )


def join(cam, mine, far, after):
    rows, half = mine.shape

    def kernel(cam_ref, mine_ref, far_ref, out_ref):
        for c, (left, right) in enumerate(((mine_ref, far_ref), (far_ref, mine_ref))):

            @pl.when(cam_ref[0] == c)
            def _():
                out_ref[:, :half] = left[...]
                out_ref[:, half:] = right[...]

    (out,), token = run(
        kernel, "join", [cam.reshape(1), mine, far], [SMEM, whole(mine), whole(far)],
        [((rows, 2 * half), BF16)], [whole((rows, 2 * half))], (1,), after,
    )
    return out, token


def copy_kernel(x_ref, out_ref):
    out_ref[...] = x_ref[...]


def copy(x, after):
    rows, width = x.shape
    steps = 4 if rows % 64 == 0 else 1
    block = pl.BlockSpec((rows // steps, width), lambda i: (i, 0))
    (out,), token = run(
        copy_kernel, "copy", [x], [block], [(x.shape, x.dtype)], [block], (steps,), after, us=1
    )
    return out, token


def project(slots, w, own, other, after):
    rows, depth = w[0].shape
    n, count = own.shape[0], len(w)

    def kernel(slot_ref, *refs):
        left = jnp.concatenate([r[...] for r in refs[:count]], 0)
        for ref, out in zip(refs[count : count + 2], refs[count + 2 :]):
            res = nt(left, ref[...]).astype(BF16)
            for j in range(count):
                out[slot_ref[j]] = res[j * rows : (j + 1) * rows]

    tokens = pl.BlockSpec((PAIR, depth), lambda i, _: (i, 0))
    return run(
        kernel, "project", [*w, own, other],
        [pl.BlockSpec((rows, depth), lambda i, _: (0, 0))] * count + [tokens] * 2,
        [((count, rows, n), BF16)] * 2, [pl.BlockSpec((count, rows, PAIR), lambda i, _: (0, 0, i))] * 2,
        (n // PAIR,), after, slots=slots, us=6,
    )


def weave(core, mine, theirs, sizes, after):
    count, rows, n = mine.shape

    def kernel(core_ref, mine_ref, theirs_ref, *outs):
        for c, (even, odd) in enumerate(((mine_ref, theirs_ref), (theirs_ref, mine_ref))):

            @pl.when(core_ref[0] == c)
            def _():
                first = 0
                for out in outs:
                    last = first + out.shape[0]
                    row = first
                    while row < last:
                        block, offset = row // rows, row % rows
                        size = min(rows - offset, last - row)
                        src = (even, odd)[block % 2]
                        out[row - first : row - first + size] = src[block // 2, offset : offset + size]
                        row += size
                    first = last

    return run(
        kernel, "weave", [core.reshape(1), mine, theirs], [SMEM, whole(mine), whole(theirs)],
        [((s * PAIR, n), BF16) for s in sizes], [whole((s * PAIR, n)) for s in sizes], (1,), after, us=2,
    )


def outer(slots, a_own, a_other, own, other, groups, after):
    _, rows, n = a_own.shape
    depth = own.shape[1]
    count, tile = sum(groups), 5 * PAIR

    def kernel(slot_ref, *refs):
        mine, theirs, (own_ref, other_ref), outs = refs[:count], refs[count : 2 * count], refs[2 * count : 2 * count + 2], refs[2 * count + 2 :]
        left = [jnp.concatenate([r[0] for r in part], 0) for part in (mine, theirs)]
        res = (mm(left[0], own_ref[...]) + mm(left[1], other_ref[...])).astype(BF16)
        first = 0
        for out in outs:
            for j in range(out.shape[0]):
                out[j] = res[(first + j) * rows : (first + j + 1) * rows]
            first += out.shape[0]

    blocks = [pl.BlockSpec((1, rows, n), lambda i, slot, j=j: (slot[j], 0, 0)) for j in range(count)]
    return run(
        kernel, "outer", [a_own] * count + [a_other] * count + [own, other],
        blocks * 2 + [pl.BlockSpec((n, tile), lambda i, _: (0, i))] * 2,
        [((g, rows, depth), BF16) for g in groups],
        [pl.BlockSpec((g, rows, tile), lambda i, _: (0, 0, i)) for g in groups],
        (pl.cdiv(depth, tile),), after, slots=slots, us=6,
    )


def add_kernel(x_ref, y_ref, *outs):
    for j, out in enumerate(outs):
        out[...] = (x_ref[j].astype(F32) + y_ref[j].astype(F32)).astype(out.dtype)


def add(x, y, dtype, after):
    count, *block = x.shape
    return run(
        add_kernel, "add", [x, y], [whole(x), whole(y)], [(tuple(block), dtype)] * count,
        [whole(tuple(block))] * count, (1,), after,
    )


def total_of(cam, parts, after):
    rows, width = parts[0].shape
    half = width // 2

    def kernel(cam_ref, *refs):
        *refs, mine, theirs = refs
        total = refs[0][...].astype(F32)
        for ref in refs[1:]:
            total += ref[...].astype(F32)
        left, right = total[:, :half], total[:, half:]
        for c, (x, y) in enumerate(((left, right), (right, left))):

            @pl.when(cam_ref[0] == c)
            def _():
                mine[...] = x
                theirs[...] = y.astype(BF16)

    return run(
        kernel, "total", [cam.reshape(1), *parts], [SMEM] + [whole(x) for x in parts],
        [((rows, half), F32), ((rows, half), BF16)], [whole((rows, half))] * 2, (1,), after,
    )


def last_sum(mine, theirs, scale, after):
    def kernel(x_ref, y_ref, out_ref):
        out_ref[...] = (x_ref[...] + y_ref[...].astype(F32)) * scale

    (out,), _ = run(
        kernel, "scale", [mine, theirs], [whole(mine)] * 2, [(mine.shape, F32)], [whole(mine)], (1,), after,
    )
    return out


def swap(x, axis, bit=1):
    size = lax.axis_size(axis)
    return lax.ppermute(x, axis, [(i, i ^ bit) for i in range(size)])


def shift(x, axis, step):
    size = lax.axis_size(axis)
    return lax.ppermute(x, axis, [(i, (i + step) % size) for i in range(size)])


def ordered(mine, theirs, flag, axis):
    return jnp.where(
        flag == 0,
        jnp.concatenate([mine, theirs], axis),
        jnp.concatenate([theirs, mine], axis),
    )


ORDER = (2, 1, 3, 0)


def body(queries, keys, values, d_out, w_out):
    shape = queries.shape
    width, model_width = shape[4], d_out.shape[4]
    n = shape[0] * shape[1] * shape[2] * shape[3]
    q, k, v = (x.reshape(n, width) for x in (queries, keys, values))
    flat = d_out.reshape(n, model_width)
    cams, bands, objs = (lax.axis_size(a) for a in ("cam", "band", "obj"))
    total = n * cams * bands * objs
    cam, band, obj = (lax.axis_index(a) for a in ("cam", "band", "obj"))
    core, line = obj % 2, obj // 2
    rows, half = w_out.shape
    blocked = bands == 4 and objs == 4
    sizes = CHUNKS if sum(CHUNKS) * PAIR == width else (1,) * (width // PAIR)
    chunks = [(sum(sizes[:i]), c) for i, c in enumerate(sizes)]

    scale = float(total) ** (-0.5)
    w_far = swap(w_out, "cam")
    sent, token = [], ()

    def send(i, after):
        packed, token = pack(k, v, *chunks[i], after)
        sent.append(swap(packed, "cam"))
        return (token,)

    def forward(i, state, after):
        state, token = attend(q, k, v, sent[i], state, *chunks[i], after)
        return state, (token,)

    def backward(i, dq, after):
        (dq, *share), token = back(state, q, k, v, d_att, dq, *parts[i], after)
        return (dq, *share), (token,)

    pairs = width // PAIR
    cuts = [pairs * i // PARTS for i in range(PARTS + 1)]
    parts = [(a, b - a) for a, b in zip(cuts, cuts[1:])]
    state, dq = (), ()
    if blocked and len(chunks) == 3 and PARTS == 2:
        flat_other = swap(flat, "obj")
        into = [2 * ((band - s) % 4) + line for s in ORDER] + [2 * ((band - s) % 4) + 1 - line for s in ORDER]
        into = jnp.stack(into).astype(jnp.int32)
        out_of = [4 * ((band + s) % 4) + 2 * (1 - line) + core for s in ORDER]
        out_of += [4 * ((band + s) % 4) + 2 * line + core for s in ORDER]
        out_of = jnp.stack(out_of).astype(jnp.int32)

        w_cols, token = join(cam, w_out, w_far, (flat_other,))
        after = send(0, (token,))
        held = [shift(w_cols, "band", s) for s in ORDER[:3]]
        passed = [None, None, None, swap(w_cols, "obj", 2)]

        def forward_w(j, after):
            x, token = copy(held[j], after)
            passed[j] = swap(x, "obj", 2)
            return (token,)

        after = send(1, (*after, passed[3]))
        state, after = forward(0, state, after)
        after = forward_w(0, after)
        after = send(2, after)
        after = forward_w(1, after)
        state, after = forward(1, state, (*after, passed[0]))
        x, token = copy(q, after)
        q_far = swap(x, "cam")
        after = forward_w(2, (token,))
        state, after = forward(2, state, (*after, passed[1]))

        a_own = state[0].reshape(bands * objs, rows, n)
        a_other = swap(a_own, "obj")
        (*away, stay), token = outer(out_of, a_own, a_other, flat, flat_other, (1, 2, 1, 4), after)
        away = [swap(x, "obj", 2) for x in away]
        (mine, theirs), token = project(into, [*held, w_cols, *passed], flat, flat_other, (token,))
        theirs = swap(theirs, "obj")
        (d_att,), token = weave(core, mine, theirs, [pairs], (token,))
        d_far = swap(d_att, "cam")
        (x,), token = add(stay[:1], away[0], BF16, (token, q_far))
        sums = [shift(x, "band", ORDER[0])]
        dq, after = backward(0, dq, (token,))
        (x, y), token = add(stay[1:3], away[1], BF16, after)
        sums += [shift(x, "band", ORDER[1]), shift(y, "band", ORDER[2])]
        (base,), token = add(stay[3:], away[2], F32, (token,))
        (dq, *share), after = backward(1, dq, (token,))
        share[2] = swap(share[2], "cam")
        (*grads,), token = cross(q_far, k, v, d_far, share, (*after, sums[0]))
        (mine, theirs), token = total_of(cam, [base, *sums], (token,))
        theirs = swap(theirs, "cam")
    else:
        after, q_far = (), swap(q, "cam")
        for i in range(len(chunks)):
            after = send(i, after)
        for i in range(len(chunks)):
            state, after = forward(i, state, after)
        full = lax.all_gather(ordered(w_out, w_far, cam, 1), ("band", "obj"), axis=0, tiled=True)
        d_att = nt(full, flat).astype(BF16)
        d_far = swap(d_att, "cam")
        for i in range(PARTS):
            dq, after = backward(i, dq, after)
        dq, *share = dq
        share[2] = swap(share[2], "cam")
        (*grads,), token = cross(q_far, k, v, d_far, share, after)
        sums = lax.psum_scatter(mm(state[0], flat), ("band", "obj"), scatter_dimension=0, tiled=True)
        mine = jnp.where(cam == 0, sums[:, :half], sums[:, half:])
        theirs = jnp.where(cam == 0, sums[:, half:], sums[:, :half])
        theirs = swap(theirs.astype(BF16), "cam")
    grad_wo = last_sum(mine, theirs, scale, (token,))
    return (dq.reshape(shape), grads[0].reshape(shape), grads[1].reshape(shape), grad_wo)


def solution(mesh):
    token = P("obj", "cam", "band", None, None)
    weight = P(("band", "obj"), "cam")
    return jax.shard_map(
        body,
        mesh=mesh,
        in_specs=(token, token, token, token, weight),
        out_specs=(token, token, token, weight),
        check_vma=False,
    )
```

```python
import jax
import jax.numpy as jnp
from jax import lax
from jax.experimental import pallas as pl
from jax.experimental.pallas import tpu as pltpu
from jax.sharding import PartitionSpec as P

BF16, F32 = jnp.bfloat16, jnp.float32
HEAD = 64
PAIR = 2 * HEAD
SCALE = HEAD**-0.5
LOG2E = 1.4426950408889634
NT = (((1,), (1,)), ((), ()))
ANY = pl.BlockSpec(memory_space=pl.ANY)
VMEM = pl.BlockSpec(memory_space=pltpu.VMEM)
SMEM = pl.BlockSpec(memory_space=pltpu.SMEM)
TOKEN = (8, 128)
BIG = 36
FLOPS_PER_US = 1150e6 * 0.5
CHUNKS = (3, 4, 3)
PARTS = (6, 3, 1)


def mm(a, b):
    return jnp.dot(a, b, preferred_element_type=F32)


def nt(a, b):
    return lax.dot_general(a, b, NT, preferred_element_type=F32)


def run(kernel, name, ins, in_specs, outs, out_specs, grid=(), after=(), alias=(), scratch=(), us=1, vmem=24, slots=None):
    hold = [*alias, *after]
    n_slots, n_in, n_hold, n_out = int(slots is not None), len(ins), len(hold), len(outs)

    def wrapped(*refs):
        last = n_slots + n_in + n_hold + n_out
        kernel(*refs[: n_slots + n_in], *refs[last - n_out : last], *refs[last + 1 :])
        refs[last][...] = jnp.zeros(TOKEN, F32)

    token_spec = pl.BlockSpec(TOKEN, lambda *_: (0, 0)) if grid else VMEM
    *results, token = pl.pallas_call(
        wrapped,
        grid_spec=pltpu.PrefetchScalarGridSpec(
            num_scalar_prefetch=n_slots,
            grid=grid,
            in_specs=[*in_specs, *[ANY] * n_hold],
            out_specs=[*out_specs, token_spec],
            scratch_shapes=list(scratch),
        ),
        out_shape=[*[jax.ShapeDtypeStruct(s, t) for s, t in outs], jax.ShapeDtypeStruct(TOKEN, F32)],
        input_output_aliases={n_slots + n_in + i: i for i in range(len(alias))},
        compiler_params=pltpu.CompilerParams(vmem_limit_bytes=vmem * 2**20),
        cost_estimate=pl.CostEstimate(flops=int(us * FLOPS_PER_US), transcendentals=0, bytes_accessed=0),
        name=name,
    )(*([] if slots is None else [slots]), *ins, *hold)
    return results, token


def whole(x):
    shape = x if isinstance(x, tuple) else x.shape
    return pl.BlockSpec(shape, lambda *_: (0,) * len(shape))


def stack_heads(x):
    lane = lax.broadcasted_iota(jnp.int32, x.shape, 1)
    zero = jnp.zeros_like(x)
    return jnp.concatenate([jnp.where(lane < HEAD, x, zero), jnp.where(lane < HEAD, zero, x)], 0)


def spread_heads(x):
    zero = jnp.zeros((HEAD, x.shape[1]), x.dtype)
    return jnp.concatenate(
        [jnp.concatenate([x[:HEAD], zero], 0), jnp.concatenate([zero, x[HEAD:]], 0)], 1
    )


def own_heads(x):
    n = x.shape[1] // 2
    return jnp.concatenate([x[:HEAD, :n], x[HEAD:, n:]], 0)


def column(n, first):
    return pl.BlockSpec((n, PAIR), lambda i: (0, first + i))


def pack_kernel(k_ref, v_ref, out_ref):
    n = k_ref.shape[0]
    out_ref[:n] = k_ref[...]
    out_ref[n:] = v_ref[...]


def pack(k, v, first, pairs, after):
    n = k.shape[0]
    (out,), token = run(
        pack_kernel, "pack", [k, v], [column(n, first)] * 2,
        [((2 * n, pairs * PAIR), BF16)], [column(2 * n, 0)], (pairs,), after, us=0.1,
    )
    return out, token


def attend_kernel(q_ref, k_ref, v_ref, kv_ref, att_ref, p_ref, stat_ref, far_ref):
    n = q_ref.shape[0]
    k = jnp.concatenate([k_ref[...], kv_ref[:n]], 0)
    v = jnp.concatenate([v_ref[...], kv_ref[n:]], 0)
    s = nt(k, stack_heads(q_ref[...]))
    top = jnp.max(s, axis=0, keepdims=True)
    e = jnp.exp2((s - top) * (SCALE * LOG2E))
    p_ref[0] = e
    inverse = 1.0 / jnp.sum(e, axis=0, keepdims=True)
    stat_ref[0] = jnp.concatenate([top, inverse], 0)
    att_ref[...] = own_heads(mm(v.T, e.astype(BF16)) * inverse).astype(BF16)
    far_ref[...] = kv_ref[...]


def attend(q, k, v, kv, state, first, pairs, after):
    n, width = q.shape
    count = width // PAIR
    at = lambda *block: pl.BlockSpec((1, *block), lambda i: (first + i, 0, 0))
    return run(
        attend_kernel, "attend",
        [q, k, v, kv], [column(n, first)] * 3 + [column(2 * n, 0)],
        [
            ((width, n), BF16), ((count, 2 * n, 2 * n), F32),
            ((count, 2, 2 * n), F32), ((2 * n, width), BF16),
        ],
        [pl.BlockSpec((PAIR, n), lambda i: (first + i, 0)), at(2 * n, 2 * n), at(2, 2 * n), column(2 * n, first)],
        (pairs,), after, state, us=1.9 * pairs, vmem=BIG,
    )


def back_kernel(p_ref, stat_ref, q_ref, k_ref, v_ref, kv_ref, d_ref, dq_ref, dk_ref, dv_ref, out_ref):
    n = q_ref.shape[0]
    k = jnp.concatenate([k_ref[...], kv_ref[:n]], 0)
    v = jnp.concatenate([v_ref[...], kv_ref[n:]], 0)
    q = stack_heads(q_ref[...])
    d = spread_heads(d_ref[...])
    p = p_ref[0] * stat_ref[0, 1:]
    dp = mm(v, d)
    delta = jnp.sum(p * dp, axis=0, keepdims=True)
    ds = (p * (dp - delta)).astype(BF16)
    dv_ref[...] = nt(p[:n].astype(BF16), d)
    dk_ref[...] = mm(ds[:n], q)
    dq_ref[...] = (own_heads(mm(k.T, ds)) * SCALE).T.astype(BF16)
    out_ref[0] = jnp.concatenate([stat_ref[0], delta], 0)


def back(state, q, k, v, d, done, first, pairs, after):
    n, width = q.shape
    _, p, stat, kv = state
    at = lambda *block: pl.BlockSpec((1, *block), lambda i: (first + i, 0, 0))
    return run(
        back_kernel, "back",
        [p, stat, q, k, v, kv, d],
        [at(2 * n, 2 * n), at(2, 2 * n)]
        + [column(n, first)] * 3
        + [column(2 * n, first), pl.BlockSpec((PAIR, n), lambda i: (first + i, 0))],
        [((n, width), BF16)] + [((n, width), F32)] * 2 + [((width // PAIR, 3, 2 * n), F32)],
        [column(n, first)] * 3 + [at(3, 2 * n)],
        (pairs,), after, done, us=2 * pairs, vmem=BIG,
    )


def cross_kernel(q_ref, k_ref, v_ref, d_ref, stat_ref, dk_ref, dv_ref, gk_ref, gv_ref):
    q = stack_heads(q_ref[...])
    d = spread_heads(d_ref[...])
    top, inverse, delta = (stat_ref[0, i : i + 1] for i in range(3))
    p = jnp.exp2((nt(k_ref[...], q) - top) * (SCALE * LOG2E)) * inverse
    ds = (p * (mm(v_ref[...], d) - delta)).astype(BF16)
    gv_ref[...] = (nt(p.astype(BF16), d) + dv_ref[...]).astype(BF16)
    gk_ref[...] = ((mm(ds, q) + dk_ref[...]) * SCALE).astype(BF16)


def cross(q, k, v, d, share, grads, first, pairs, after):
    n, width = q.shape
    dk, dv, stat = share
    return run(
        cross_kernel, "cross",
        [q, k, v, d, stat, dk, dv],
        [column(n, first)] * 3
        + [pl.BlockSpec((PAIR, n), lambda i: (first + i, 0)), pl.BlockSpec((1, 3, 2 * n), lambda i: (first + i, 0, 0))]
        + [column(n, first)] * 2,
        [((n, width), BF16)] * 2, [column(n, first)] * 2, (pairs,), after, grads, us=1.5 * pairs, vmem=BIG,
    )


def join(cam, mine, far, after):
    rows, half = mine.shape

    def kernel(cam_ref, mine_ref, far_ref, out_ref):
        for c, (left, right) in enumerate(((mine_ref, far_ref), (far_ref, mine_ref))):

            @pl.when(cam_ref[0] == c)
            def _():
                out_ref[:, :half] = left[...]
                out_ref[:, half:] = right[...]

    (out,), token = run(
        kernel, "join", [cam.reshape(1), mine, far], [SMEM, whole(mine), whole(far)],
        [((rows, 2 * half), BF16)], [whole((rows, 2 * half))], (1,), after, us=30,
    )
    return out, token


def copy(parts, after):
    rows, width = parts[0].shape
    count = len(parts)

    def kernel(*refs):
        for i, ref in enumerate(refs[:count]):
            refs[count][i * rows : (i + 1) * rows] = ref[...]

    (out,), token = run(
        kernel, "copy", parts, [whole(x) for x in parts],
        [((count * rows, width), BF16)], [whole((count * rows, width))], (1,), after, us=1,
    )
    return out, token


def project(w, own, other, after):
    rows, depth = w[0].shape
    n, parts, count = own.shape[0], len(w), sum(x.shape[0] for x in w) // rows

    def kernel(*refs):
        left = jnp.concatenate([r[...] for r in refs[:parts]], 0)
        for ref, out in zip(refs[parts : parts + 2], refs[parts + 2 :]):
            res = nt(left, ref[...]).astype(BF16)
            for j in range(count):
                out[j] = res[j * rows : (j + 1) * rows]

    tokens = pl.BlockSpec((PAIR, depth), lambda i: (i, 0))
    return run(
        kernel, "project", [*w, own, other],
        [whole(x) for x in w] + [tokens] * 2,
        [((count, rows, n), BF16)] * 2, [pl.BlockSpec((count, rows, PAIR), lambda i: (0, 0, i))] * 2,
        (n // PAIR,), after, us=count - 1.9,
    )


def weave(core, slots, mine, theirs, after):
    _, rows, n = mine[0].shape
    total = 2 * slots.shape[0]

    def kernel(slot_ref, core_ref, *refs):
        *refs, out = refs
        for side, which in enumerate((core_ref[0], 1 - core_ref[0])):
            place = 0
            for ref in refs[side * len(mine) : (side + 1) * len(mine)]:
                for j in range(ref.shape[0]):
                    out[2 * slot_ref[place] + which] = ref[j]
                    place += 1

    ins = [slots, core.reshape(1), *mine, *theirs]
    (out,), token = run(
        kernel, "weave", ins, [SMEM, SMEM] + [whole(x) for x in (*mine, *theirs)],
        [((total, rows, n), BF16)], [whole((total, rows, n))], (1,), after, us=2,
    )
    return out.reshape(total * rows, n), token


def outer(slots, a_own, a_other, own, other, groups, after):
    _, rows, n = a_own.shape
    depth = own.shape[1]
    count, tile = sum(groups), 5 * PAIR

    def kernel(slot_ref, *refs):
        mine, theirs, (own_ref, other_ref), outs = refs[:count], refs[count : 2 * count], refs[2 * count : 2 * count + 2], refs[2 * count + 2 :]
        left = [jnp.concatenate([r[0] for r in part], 0) for part in (mine, theirs)]
        right = jnp.concatenate([own_ref[...], other_ref[...]], 0)
        res = mm(jnp.concatenate(left, 1), right).astype(BF16)
        first = 0
        for out in outs:
            for j in range(out.shape[0]):
                out[j] = res[(first + j) * rows : (first + j + 1) * rows]
            first += out.shape[0]

    blocks = [pl.BlockSpec((1, rows, n), lambda i, slot, j=j: (slot[j], 0, 0)) for j in range(count)]
    return run(
        kernel, "outer", [a_own] * count + [a_other] * count + [own, other],
        blocks * 2 + [pl.BlockSpec((n, tile), lambda i, _: (0, i))] * 2,
        [((g, rows, depth), BF16) for g in groups],
        [pl.BlockSpec((g, rows, tile), lambda i, _: (0, 0, i)) for g in groups],
        (pl.cdiv(depth, tile),), after, slots=slots, us=6,
    )


def add_kernel(x_ref, y_ref, *outs):
    for j, out in enumerate(outs):
        out[...] = (x_ref[j].astype(F32) + y_ref[j].astype(F32)).astype(out.dtype)


def add(x, y, types, after):
    count, *block = x.shape
    return run(
        add_kernel, "add", [x, y], [whole(x), whole(y)], [(tuple(block), t) for t in types],
        [whole(tuple(block))] * count, (1,), after,
    )


def total_of(cam, parts, after):
    rows, width = parts[0].shape
    half = width // 2

    def kernel(cam_ref, *refs):
        *refs, mine, theirs = refs
        total = refs[0][...].astype(F32)
        for ref in refs[1:]:
            total += ref[...].astype(F32)
        left, right = total[:, :half], total[:, half:]
        for c, (x, y) in enumerate(((left, right), (right, left))):

            @pl.when(cam_ref[0] == c)
            def _():
                mine[...] = x
                theirs[...] = y.astype(BF16)

    return run(
        kernel, "total", [cam.reshape(1), *parts], [SMEM] + [whole(x) for x in parts],
        [((rows, half), F32), ((rows, half), BF16)], [whole((rows, half))] * 2, (1,), after,
    )


def last_sum(mine, theirs, scale, after):
    def kernel(x_ref, y_ref, out_ref):
        out_ref[...] = (x_ref[...] + y_ref[...].astype(F32)) * scale

    (out,), _ = run(
        kernel, "scale", [mine, theirs], [whole(mine)] * 2, [(mine.shape, F32)], [whole(mine)], (1,), after,
    )
    return out


def swap(x, axis, bit=1):
    size = lax.axis_size(axis)
    return lax.ppermute(x, axis, [(i, i ^ bit) for i in range(size)])


def shift(x, axis, step):
    size = lax.axis_size(axis)
    return lax.ppermute(x, axis, [(i, (i + step) % size) for i in range(size)])


def ordered(mine, theirs, flag, axis):
    return jnp.where(
        flag == 0,
        jnp.concatenate([mine, theirs], axis),
        jnp.concatenate([theirs, mine], axis),
    )


ORDER = (1, 3, 2)
LATE = (2, 1, 3, 0)


def body(queries, keys, values, d_out, w_out):
    shape = queries.shape
    width, model_width = shape[4], d_out.shape[4]
    n = shape[0] * shape[1] * shape[2] * shape[3]
    q, k, v = (x.reshape(n, width) for x in (queries, keys, values))
    flat = d_out.reshape(n, model_width)
    cams, bands, objs = (lax.axis_size(a) for a in ("cam", "band", "obj"))
    total = n * cams * bands * objs
    cam, band, obj = (lax.axis_index(a) for a in ("cam", "band", "obj"))
    core, line = obj % 2, obj // 2
    rows, half = w_out.shape
    blocked = bands == 4 and objs == 4
    sizes = CHUNKS if sum(CHUNKS) * PAIR == width else (1,) * (width // PAIR)
    chunks = [(sum(sizes[:i]), c) for i, c in enumerate(sizes)]

    scale = float(total) ** (-0.5)
    w_far = swap(w_out, "cam")
    sent, token = [], ()

    def send(i, after):
        packed, token = pack(k, v, *chunks[i], after)
        sent.append(swap(packed, "cam"))
        return (token,)

    def forward(i, state, after):
        state, token = attend(q, k, v, sent[i], state, *chunks[i], after)
        return state, (token,)

    def backward(i, dq, after):
        (dq, *share), token = back(state, q, k, v, d_att, dq, *parts[i], after)
        return (dq, *share), (token,)

    pairs = width // PAIR
    parts = [(sum(PARTS[:i]), c) for i, c in enumerate(PARTS)] if sum(PARTS) == pairs else [(0, pairs)]
    state, dq = (), ()
    if blocked and len(chunks) == len(parts) == 3:
        flat_other = swap(flat, "obj")
        into = [2 * band + line, 2 * band + 1 - line]
        into += [2 * ((band - s) % 4) + l for l in (line, 1 - line) for s in ORDER]
        into = jnp.stack(into).astype(jnp.int32)
        out_of = [4 * ((band + s) % 4) + 2 * l + core for l in (1 - line, line) for s in LATE]
        out_of = jnp.stack(out_of).astype(jnp.int32)

        after = send(0, ())
        w_cols, token = join(cam, w_out, w_far, after)
        held = [shift(w_cols, "band", s) for s in ORDER]
        y_own = swap(w_cols, "obj", 2)
        after = send(1, (token, flat_other))
        (mine_a, theirs_a), token = project([w_cols, y_own], flat, flat_other, after)
        theirs_a = swap(theirs_a, "obj")
        state, after = forward(0, state, (token,))
        x, token = copy(held[:2], after)
        y_near = swap(x, "obj", 2)
        after = send(2, (token,))
        state, after = forward(1, state, after)
        x, token = copy([q], after)
        q_far = swap(x, "cam")
        x, token = copy(held[2:], (token, y_near))
        y_far = swap(x, "obj", 2)
        state, after = forward(2, state, (token,))

        a_own = state[0].reshape(bands * objs, rows, n)
        a_other = swap(a_own, "obj")
        (*away, stay), token = outer(out_of, a_own, a_other, flat, flat_other, (1, 1, 2, 4), after)
        away = [swap(x, "obj", 2) for x in away]
        (mine_b, theirs_b), token = project([*held, y_near, y_far], flat, flat_other, (token,))
        theirs_b = swap(theirs_b, "obj")
        (x,), token = add(stay[:1], away[0], (BF16,), (token,))
        sums = [shift(x, "band", LATE[0])]
        d_att, token = weave(core, into, [mine_a, mine_b], [theirs_a, theirs_b], (token, q_far))
        d_far = swap(d_att, "cam")
        dq, after = backward(0, dq, (token,))
        (x,), token = add(stay[1:2], away[1], (BF16,), after)
        sums.append(shift(x, "band", LATE[1]))
        dq, after = backward(1, dq, (token,))
        (dq, *share), after = backward(2, dq, (*after, sums[0]))
        share[2] = swap(share[2], "cam")
        (x, base), token = add(stay[2:], away[2], (BF16, F32), after)
        sums.append(shift(x, "band", LATE[2]))
        grads, token = cross(q_far, k, v, d_far, share, (), 0, pairs // 2, (token, sums[1]))
        (mine, theirs), token = total_of(cam, [base, *sums], (token,))
        theirs = swap(theirs, "cam")
        grads, token = cross(q_far, k, v, d_far, share, grads, pairs // 2, pairs - pairs // 2, (token,))
    else:
        after, q_far = (), swap(q, "cam")
        for i in range(len(chunks)):
            after = send(i, after)
        for i in range(len(chunks)):
            state, after = forward(i, state, after)
        full = lax.all_gather(ordered(w_out, w_far, cam, 1), ("band", "obj"), axis=0, tiled=True)
        d_att = nt(full, flat).astype(BF16)
        d_far = swap(d_att, "cam")
        for i in range(len(parts)):
            dq, after = backward(i, dq, after)
        dq, *share = dq
        share[2] = swap(share[2], "cam")
        grads, token = cross(q_far, k, v, d_far, share, (), 0, pairs, after)
        sums = lax.psum_scatter(mm(state[0], flat), ("band", "obj"), scatter_dimension=0, tiled=True)
        mine = jnp.where(cam == 0, sums[:, :half], sums[:, half:])
        theirs = jnp.where(cam == 0, sums[:, half:], sums[:, :half])
        theirs = swap(theirs.astype(BF16), "cam")
    grad_wo = last_sum(mine, theirs, scale, (token,))
    return (dq.reshape(shape), grads[0].reshape(shape), grads[1].reshape(shape), grad_wo)


def solution(mesh):
    token = P("obj", "cam", "band", None, None)
    weight = P(("band", "obj"), "cam")
    return jax.shard_map(
        body,
        mesh=mesh,
        in_specs=(token, token, token, token, weight),
        out_specs=(token, token, token, weight),
        check_vma=False,
    )
```

```python
import jax
import jax.numpy as jnp
from jax import lax
from jax.experimental import pallas as pl
from jax.experimental.pallas import tpu as pltpu
from jax.sharding import PartitionSpec as P

BF16, F32 = jnp.bfloat16, jnp.float32
HEAD = 64
PAIR = 2 * HEAD
SCALE = HEAD**-0.5
LOG2E = 1.4426950408889634
NT = (((1,), (1,)), ((), ()))
ANY = pl.BlockSpec(memory_space=pl.ANY)
VMEM = pl.BlockSpec(memory_space=pltpu.VMEM)
SMEM = pl.BlockSpec(memory_space=pltpu.SMEM)
TOKEN = (8, 128)
BIG = 36
FLOPS_PER_US = 1150e6 * 0.5
CHUNKS = (3, 4, 3)
PARTS = (6, 3, 1)


def mm(a, b):
    return jnp.dot(a, b, preferred_element_type=F32)


def nt(a, b):
    return lax.dot_general(a, b, NT, preferred_element_type=F32)


def run(kernel, name, ins, in_specs, outs, out_specs, grid=(), after=(), alias=(), scratch=(), us=1, vmem=24, slots=None):
    hold = [*alias, *after]
    n_slots, n_in, n_hold, n_out = int(slots is not None), len(ins), len(hold), len(outs)

    def wrapped(*refs):
        last = n_slots + n_in + n_hold + n_out
        kernel(*refs[: n_slots + n_in], *refs[last - n_out : last], *refs[last + 1 :])
        refs[last][...] = jnp.zeros(TOKEN, F32)

    token_spec = pl.BlockSpec(TOKEN, lambda *_: (0, 0)) if grid else VMEM
    *results, token = pl.pallas_call(
        wrapped,
        grid_spec=pltpu.PrefetchScalarGridSpec(
            num_scalar_prefetch=n_slots,
            grid=grid,
            in_specs=[*in_specs, *[ANY] * n_hold],
            out_specs=[*out_specs, token_spec],
            scratch_shapes=list(scratch),
        ),
        out_shape=[*[jax.ShapeDtypeStruct(s, t) for s, t in outs], jax.ShapeDtypeStruct(TOKEN, F32)],
        input_output_aliases={n_slots + n_in + i: i for i in range(len(alias))},
        compiler_params=pltpu.CompilerParams(vmem_limit_bytes=vmem * 2**20),
        cost_estimate=pl.CostEstimate(flops=int(us * FLOPS_PER_US), transcendentals=0, bytes_accessed=0),
        name=name,
    )(*([] if slots is None else [slots]), *ins, *hold)
    return results, token


def whole(x):
    shape = x if isinstance(x, tuple) else x.shape
    return pl.BlockSpec(shape, lambda *_: (0,) * len(shape))


def stack_heads(x):
    lane = lax.broadcasted_iota(jnp.int32, x.shape, 1)
    zero = jnp.zeros_like(x)
    return jnp.concatenate([jnp.where(lane < HEAD, x, zero), jnp.where(lane < HEAD, zero, x)], 0)


def spread_heads(x):
    zero = jnp.zeros((HEAD, x.shape[1]), x.dtype)
    return jnp.concatenate(
        [jnp.concatenate([x[:HEAD], zero], 0), jnp.concatenate([zero, x[HEAD:]], 0)], 1
    )


def own_heads(x):
    n = x.shape[1] // 2
    return jnp.concatenate([x[:HEAD, :n], x[HEAD:, n:]], 0)


def column(n, first):
    return pl.BlockSpec((n, PAIR), lambda i: (0, first + i))


def pack_kernel(k_ref, v_ref, out_ref):
    n = k_ref.shape[0]
    out_ref[:n] = k_ref[...]
    out_ref[n:] = v_ref[...]


def pack(k, v, first, pairs, after):
    n = k.shape[0]
    (out,), token = run(
        pack_kernel, "pack", [k, v], [column(n, first)] * 2,
        [((2 * n, pairs * PAIR), BF16)], [column(2 * n, 0)], (pairs,), after, us=0.1,
    )
    return out, token


def attend_kernel(q_ref, k_ref, v_ref, kv_ref, att_ref, p_ref, stat_ref, far_ref):
    n = q_ref.shape[0]
    k = jnp.concatenate([k_ref[...], kv_ref[:n]], 0)
    v = jnp.concatenate([v_ref[...], kv_ref[n:]], 0)
    s = nt(k, stack_heads(q_ref[...]))
    top = jnp.max(s, axis=0, keepdims=True)
    e = jnp.exp2((s - top) * (SCALE * LOG2E)).astype(BF16)
    p_ref[0] = e
    inverse = 1.0 / jnp.sum(e.astype(F32), axis=0, keepdims=True)
    stat_ref[0] = jnp.concatenate([top, inverse], 0)
    att_ref[...] = own_heads(mm(v.T, e) * inverse).astype(BF16)
    far_ref[...] = kv_ref[...]


def attend(q, k, v, kv, state, first, pairs, after):
    n, width = q.shape
    count = width // PAIR
    at = lambda *block: pl.BlockSpec((1, *block), lambda i: (first + i, 0, 0))
    return run(
        attend_kernel, "attend",
        [q, k, v, kv], [column(n, first)] * 3 + [column(2 * n, 0)],
        [
            ((width, n), BF16), ((2 * count, 2 * n, 2 * n), BF16),
            ((count, 2, 2 * n), F32), ((2 * n, width), BF16),
        ],
        [pl.BlockSpec((PAIR, n), lambda i: (first + i, 0)), at(2 * n, 2 * n), at(2, 2 * n), column(2 * n, first)],
        (pairs,), after, state, us=0.4 * pairs, vmem=BIG,
    )


def back_kernel(p_ref, stat_ref, q_ref, k_ref, v_ref, kv_ref, d_ref, dq_ref, dk_ref, dv_ref, out_ref):
    n = q_ref.shape[0]
    k = jnp.concatenate([k_ref[...], kv_ref[:n]], 0)
    v = jnp.concatenate([v_ref[...], kv_ref[n:]], 0)
    q = stack_heads(q_ref[...])
    d = spread_heads(d_ref[...])
    p = p_ref[0].astype(F32) * stat_ref[0, 1:]
    dp = mm(v, d)
    delta = jnp.sum(p * dp, axis=0, keepdims=True)
    ds = (p * (dp - delta)).astype(BF16)
    dv_ref[...] = nt(p[:n].astype(BF16), d)
    dk_ref[...] = mm(ds[:n], q)
    dq_ref[...] = (own_heads(mm(k.T, ds)) * SCALE).T.astype(BF16)
    out_ref[0] = jnp.concatenate([stat_ref[0], delta], 0)


def back(state, q, k, v, d, done, first, pairs, after):
    n, width = q.shape
    _, p, stat, kv = state
    at = lambda *block: pl.BlockSpec((1, *block), lambda i: (first + i, 0, 0))
    return run(
        back_kernel, "back",
        [p, stat, q, k, v, kv, d],
        [at(2 * n, 2 * n), at(2, 2 * n)]
        + [column(n, first)] * 3
        + [column(2 * n, first), pl.BlockSpec((PAIR, n), lambda i: (first + i, 0))],
        [((n, width), BF16)] + [((n, width), F32)] * 2 + [((width // PAIR, 3, 2 * n), F32)],
        [column(n, first)] * 3 + [at(3, 2 * n)],
        (pairs,), after, done, us=0.1 if first else 2 * pairs, vmem=BIG,
    )


def cross_kernel(q_ref, k_ref, v_ref, d_ref, stat_ref, dk_ref, dv_ref, gk_ref, gv_ref):
    q = stack_heads(q_ref[...])
    d = spread_heads(d_ref[...])
    top, inverse, delta = (stat_ref[0, i : i + 1] for i in range(3))
    e = jnp.exp2((nt(k_ref[...], q) - top) * (SCALE * LOG2E)).astype(BF16)
    p = e.astype(F32) * inverse
    ds = (p * (mm(v_ref[...], d) - delta)).astype(BF16)
    gv_ref[...] = (nt(p.astype(BF16), d) + dv_ref[...]).astype(BF16)
    gk_ref[...] = ((mm(ds, q) + dk_ref[...]) * SCALE).astype(BF16)


def cross(q, k, v, d, share, grads, first, pairs, after):
    n, width = q.shape
    dk, dv, stat = share
    return run(
        cross_kernel, "cross",
        [q, k, v, d, stat, dk, dv],
        [column(n, first)] * 3
        + [pl.BlockSpec((PAIR, n), lambda i: (first + i, 0)), pl.BlockSpec((1, 3, 2 * n), lambda i: (first + i, 0, 0))]
        + [column(n, first)] * 2,
        [((n, width), BF16)] * 2, [column(n, first)] * 2, (pairs,), after, grads, us=1.5 * pairs, vmem=BIG,
    )


def join(cam, mine, far, after):
    rows, half = mine.shape

    def kernel(cam_ref, mine_ref, far_ref, out_ref):
        for c, (left, right) in enumerate(((mine_ref, far_ref), (far_ref, mine_ref))):

            @pl.when(cam_ref[0] == c)
            def _():
                out_ref[:, :half] = left[...]
                out_ref[:, half:] = right[...]

    (out,), token = run(
        kernel, "join", [cam.reshape(1), mine, far], [SMEM, whole(mine), whole(far)],
        [((rows, 2 * half), BF16)], [whole((rows, 2 * half))], (1,), after, us=30,
    )
    return out, token


def copy(parts, after):
    rows, width = parts[0].shape
    count = len(parts)

    def kernel(*refs):
        for i, ref in enumerate(refs[:count]):
            refs[count][i * rows : (i + 1) * rows] = ref[...]

    (out,), token = run(
        kernel, "copy", parts, [whole(x) for x in parts],
        [((count * rows, width), BF16)], [whole((count * rows, width))], (1,), after, us=1,
    )
    return out, token


def project(w, own, other, after):
    rows, depth = w[0].shape
    n, parts, count = own.shape[0], len(w), sum(x.shape[0] for x in w) // rows

    def kernel(*refs):
        left = jnp.concatenate([r[...] for r in refs[:parts]], 0)
        for ref, out in zip(refs[parts : parts + 2], refs[parts + 2 :]):
            res = nt(left, ref[...]).astype(BF16)
            for j in range(count):
                out[j] = res[j * rows : (j + 1) * rows]

    tokens = pl.BlockSpec((PAIR, depth), lambda i: (i, 0))
    return run(
        kernel, "project", [*w, own, other],
        [whole(x) for x in w] + [tokens] * 2,
        [((count, rows, n), BF16)] * 2, [pl.BlockSpec((count, rows, PAIR), lambda i: (0, 0, i))] * 2,
        (n // PAIR,), after, us=count - 1.9,
    )


def weave(core, slots, mine, theirs, after):
    _, rows, n = mine[0].shape
    total = 2 * slots.shape[0]

    def kernel(slot_ref, core_ref, *refs):
        *refs, out = refs
        for side, which in enumerate((core_ref[0], 1 - core_ref[0])):
            place = 0
            for ref in refs[side * len(mine) : (side + 1) * len(mine)]:
                for j in range(ref.shape[0]):
                    out[2 * slot_ref[place] + which] = ref[j]
                    place += 1

    ins = [slots, core.reshape(1), *mine, *theirs]
    (out,), token = run(
        kernel, "weave", ins, [SMEM, SMEM] + [whole(x) for x in (*mine, *theirs)],
        [((total, rows, n), BF16)], [whole((total, rows, n))], (1,), after, us=2,
    )
    return out.reshape(total * rows, n), token


def outer(slots, a_own, a_other, own, other, groups, after):
    _, rows, n = a_own.shape
    depth = own.shape[1]
    count, tile = sum(groups), 5 * PAIR

    def kernel(slot_ref, *refs):
        mine, theirs, (own_ref, other_ref), outs = refs[:count], refs[count : 2 * count], refs[2 * count : 2 * count + 2], refs[2 * count + 2 :]
        left = [jnp.concatenate([r[0] for r in part], 0) for part in (mine, theirs)]
        right = jnp.concatenate([own_ref[...], other_ref[...]], 0)
        res = mm(jnp.concatenate(left, 1), right).astype(BF16)
        first = 0
        for out in outs:
            for j in range(out.shape[0]):
                out[j] = res[(first + j) * rows : (first + j + 1) * rows]
            first += out.shape[0]

    blocks = [pl.BlockSpec((1, rows, n), lambda i, slot, j=j: (slot[j], 0, 0)) for j in range(count)]
    return run(
        kernel, "outer", [a_own] * count + [a_other] * count + [own, other],
        blocks * 2 + [pl.BlockSpec((n, tile), lambda i, _: (0, i))] * 2,
        [((g, rows, depth), BF16) for g in groups],
        [pl.BlockSpec((g, rows, tile), lambda i, _: (0, 0, i)) for g in groups],
        (pl.cdiv(depth, tile),), after, slots=slots, us=6,
    )


def add_kernel(x_ref, y_ref, *outs):
    for j, out in enumerate(outs):
        out[...] = (x_ref[j].astype(F32) + y_ref[j].astype(F32)).astype(out.dtype)


def add(x, y, types, after):
    count, *block = x.shape
    return run(
        add_kernel, "add", [x, y], [whole(x), whole(y)], [(tuple(block), t) for t in types],
        [whole(tuple(block))] * count, (1,), after,
    )


def total_of(cam, parts, after):
    rows, width = parts[0].shape
    half = width // 2

    def kernel(cam_ref, *refs):
        *refs, mine, theirs = refs
        total = refs[0][...].astype(F32)
        for ref in refs[1:]:
            total += ref[...].astype(F32)
        left, right = total[:, :half], total[:, half:]
        for c, (x, y) in enumerate(((left, right), (right, left))):

            @pl.when(cam_ref[0] == c)
            def _():
                mine[...] = x
                theirs[...] = y.astype(BF16)

    return run(
        kernel, "total", [cam.reshape(1), *parts], [SMEM] + [whole(x) for x in parts],
        [((rows, half), F32), ((rows, half), BF16)], [whole((rows, half))] * 2, (1,), after,
    )


def last_sum(mine, theirs, scale, after):
    def kernel(x_ref, y_ref, out_ref):
        out_ref[...] = (x_ref[...] + y_ref[...].astype(F32)) * scale

    (out,), _ = run(
        kernel, "scale", [mine, theirs], [whole(mine)] * 2, [(mine.shape, F32)], [whole(mine)], (1,), after,
    )
    return out


def swap(x, axis, bit=1):
    size = lax.axis_size(axis)
    return lax.ppermute(x, axis, [(i, i ^ bit) for i in range(size)])


def shift(x, axis, step):
    size = lax.axis_size(axis)
    return lax.ppermute(x, axis, [(i, (i + step) % size) for i in range(size)])


def ordered(mine, theirs, flag, axis):
    return jnp.where(
        flag == 0,
        jnp.concatenate([mine, theirs], axis),
        jnp.concatenate([theirs, mine], axis),
    )


ORDER = (1, 3, 2)
LATE = (2, 1, 3, 0)


def body(queries, keys, values, d_out, w_out):
    shape = queries.shape
    width, model_width = shape[4], d_out.shape[4]
    n = shape[0] * shape[1] * shape[2] * shape[3]
    q, k, v = (x.reshape(n, width) for x in (queries, keys, values))
    flat = d_out.reshape(n, model_width)
    cams, bands, objs = (lax.axis_size(a) for a in ("cam", "band", "obj"))
    total = n * cams * bands * objs
    cam, band, obj = (lax.axis_index(a) for a in ("cam", "band", "obj"))
    core, line = obj % 2, obj // 2
    rows, half = w_out.shape
    blocked = bands == 4 and objs == 4
    sizes = CHUNKS if sum(CHUNKS) * PAIR == width else (1,) * (width // PAIR)
    chunks = [(sum(sizes[:i]), c) for i, c in enumerate(sizes)]

    scale = float(total) ** (-0.5)
    w_far = swap(w_out, "cam")
    sent, token = [], ()

    def send(i, after):
        packed, token = pack(k, v, *chunks[i], after)
        sent.append(swap(packed, "cam"))
        return (token,)

    def forward(i, state, after):
        state, token = attend(q, k, v, sent[i], state, *chunks[i], after)
        return state, (token,)

    def backward(i, dq, after):
        (dq, *share), token = back(state, q, k, v, d_att, dq, *parts[i], after)
        return (dq, *share), (token,)

    pairs = width // PAIR
    parts = [(sum(PARTS[:i]), c) for i, c in enumerate(PARTS)] if sum(PARTS) == pairs else [(0, pairs)]
    state, dq = (), ()
    if blocked and len(chunks) == len(parts) == 3:
        flat_other = swap(flat, "obj")
        into = [2 * band + line, 2 * band + 1 - line]
        into += [2 * ((band - s) % 4) + l for l in (line, 1 - line) for s in ORDER]
        into = jnp.stack(into).astype(jnp.int32)
        out_of = [4 * ((band + s) % 4) + 2 * l + core for l in (1 - line, line) for s in LATE]
        out_of = jnp.stack(out_of).astype(jnp.int32)

        after = send(0, ())
        w_cols, token = join(cam, w_out, w_far, after)
        held = [shift(w_cols, "band", s) for s in ORDER]
        y_own = swap(w_cols, "obj", 2)
        after = send(1, (token, flat_other))
        (mine_a, theirs_a), token = project([w_cols, y_own], flat, flat_other, after)
        theirs_a = swap(theirs_a, "obj")
        state, after = forward(0, state, (token,))
        x, token = copy(held[:2], after)
        y_near = swap(x, "obj", 2)
        after = send(2, (token,))
        state, after = forward(1, state, after)
        x, token = copy([q], after)
        q_far = swap(x, "cam")
        x, token = copy(held[2:], (token, y_near))
        y_far = swap(x, "obj", 2)
        state, after = forward(2, state, (token,))

        a_own = state[0].reshape(bands * objs, rows, n)
        a_other = swap(a_own, "obj")
        (*away, stay), token = outer(out_of, a_own, a_other, flat, flat_other, (1, 1, 2, 4), after)
        away = [swap(x, "obj", 2) for x in away]
        (mine_b, theirs_b), token = project([*held, y_near, y_far], flat, flat_other, (token,))
        theirs_b = swap(theirs_b, "obj")
        (x,), token = add(stay[:1], away[0], (BF16,), (token,))
        sums = [shift(x, "band", LATE[0])]
        d_att, token = weave(core, into, [mine_a, mine_b], [theirs_a, theirs_b], (token, q_far))
        d_far = swap(d_att, "cam")
        dq, after = backward(0, dq, (token,))
        (x,), token = add(stay[1:2], away[1], (BF16,), after)
        sums.append(shift(x, "band", LATE[1]))
        dq, after = backward(1, dq, (token,))
        (dq, *share), after = backward(2, dq, after)
        share[2] = swap(share[2], "cam")
        (x, base), token = add(stay[2:], away[2], (BF16, F32), (*after, sums[0]))
        sums.append(shift(x, "band", LATE[2]))
        grads, token = cross(q_far, k, v, d_far, share, (), 0, pairs // 2, (token, sums[1]))
        (mine, theirs), token = total_of(cam, [base, *sums], (token,))
        theirs = swap(theirs, "cam")
        grads, token = cross(q_far, k, v, d_far, share, grads, pairs // 2, pairs - pairs // 2, (token,))
    else:
        after, q_far = (), swap(q, "cam")
        for i in range(len(chunks)):
            after = send(i, after)
        for i in range(len(chunks)):
            state, after = forward(i, state, after)
        full = lax.all_gather(ordered(w_out, w_far, cam, 1), ("band", "obj"), axis=0, tiled=True)
        d_att = nt(full, flat).astype(BF16)
        d_far = swap(d_att, "cam")
        for i in range(len(parts)):
            dq, after = backward(i, dq, after)
        dq, *share = dq
        share[2] = swap(share[2], "cam")
        grads, token = cross(q_far, k, v, d_far, share, (), 0, pairs, after)
        sums = lax.psum_scatter(mm(state[0], flat), ("band", "obj"), scatter_dimension=0, tiled=True)
        mine = jnp.where(cam == 0, sums[:, :half], sums[:, half:])
        theirs = jnp.where(cam == 0, sums[:, half:], sums[:, :half])
        theirs = swap(theirs.astype(BF16), "cam")
    grad_wo = last_sum(mine, theirs, scale, (token,))
    return (dq.reshape(shape), grads[0].reshape(shape), grads[1].reshape(shape), grad_wo)


def solution(mesh):
    token = P("obj", "cam", "band", None, None)
    weight = P(("band", "obj"), "cam")
    return jax.shard_map(
        body,
        mesh=mesh,
        in_specs=(token, token, token, token, weight),
        out_specs=(token, token, token, weight),
        check_vma=False,
    )
```

```python
import jax
import jax.numpy as jnp
from jax import lax
from jax.experimental import pallas as pl
from jax.experimental.pallas import tpu as pltpu
from jax.sharding import PartitionSpec as P

BF16, F32 = jnp.bfloat16, jnp.float32
HEAD = 64
PAIR = 2 * HEAD
SCALE = HEAD**-0.5
LOG2E = 1.4426950408889634
NT = (((1,), (1,)), ((), ()))
ANY = pl.BlockSpec(memory_space=pl.ANY)
VMEM = pl.BlockSpec(memory_space=pltpu.VMEM)
SMEM = pl.BlockSpec(memory_space=pltpu.SMEM)
TOKEN = (8, 128)
BIG = 36
FLOPS_PER_US = 1150e6 * 0.5
CHUNKS = (3, 5, 2)
PARTS = (6, 3, 1)


def mm(a, b):
    return jnp.dot(a, b, preferred_element_type=F32)


def nt(a, b):
    return lax.dot_general(a, b, NT, preferred_element_type=F32)


def run(kernel, name, ins, in_specs, outs, out_specs, grid=(), after=(), alias=(), scratch=(), us=1, vmem=24, slots=None):
    hold = [*alias, *after]
    n_slots, n_in, n_hold, n_out = int(slots is not None), len(ins), len(hold), len(outs)

    def wrapped(*refs):
        last = n_slots + n_in + n_hold + n_out
        kernel(*refs[: n_slots + n_in], *refs[last - n_out : last], *refs[last + 1 :])
        refs[last][...] = jnp.zeros(TOKEN, F32)

    token_spec = pl.BlockSpec(TOKEN, lambda *_: (0, 0)) if grid else VMEM
    *results, token = pl.pallas_call(
        wrapped,
        grid_spec=pltpu.PrefetchScalarGridSpec(
            num_scalar_prefetch=n_slots,
            grid=grid,
            in_specs=[*in_specs, *[ANY] * n_hold],
            out_specs=[*out_specs, token_spec],
            scratch_shapes=list(scratch),
        ),
        out_shape=[*[jax.ShapeDtypeStruct(s, t) for s, t in outs], jax.ShapeDtypeStruct(TOKEN, F32)],
        input_output_aliases={n_slots + n_in + i: i for i in range(len(alias))},
        compiler_params=pltpu.CompilerParams(vmem_limit_bytes=vmem * 2**20),
        cost_estimate=pl.CostEstimate(flops=int(us * FLOPS_PER_US), transcendentals=0, bytes_accessed=0),
        name=name,
    )(*([] if slots is None else [slots]), *ins, *hold)
    return results, token


def whole(x):
    shape = x if isinstance(x, tuple) else x.shape
    return pl.BlockSpec(shape, lambda *_: (0,) * len(shape))


def stack_heads(x):
    lane = lax.broadcasted_iota(jnp.int32, x.shape, 1)
    zero = jnp.zeros_like(x)
    return jnp.concatenate([jnp.where(lane < HEAD, x, zero), jnp.where(lane < HEAD, zero, x)], 0)


def spread_heads(x):
    zero = jnp.zeros((HEAD, x.shape[1]), x.dtype)
    return jnp.concatenate(
        [jnp.concatenate([x[:HEAD], zero], 0), jnp.concatenate([zero, x[HEAD:]], 0)], 1
    )


def own_heads(x):
    n = x.shape[1] // 2
    return jnp.concatenate([x[:HEAD, :n], x[HEAD:, n:]], 0)


def column(n, first):
    return pl.BlockSpec((n, PAIR), lambda i: (0, first + i))


def pack_kernel(k_ref, v_ref, out_ref):
    n = k_ref.shape[0]
    out_ref[:n] = k_ref[...]
    out_ref[n:] = v_ref[...]


def pack(k, v, first, pairs, after):
    n = k.shape[0]
    (out,), token = run(
        pack_kernel, "pack", [k, v], [column(n, first)] * 2,
        [((2 * n, pairs * PAIR), BF16)], [column(2 * n, 0)], (pairs,), after, us=0.1,
    )
    return out, token


def attend_kernel(q_ref, k_ref, v_ref, kv_ref, att_ref, p_ref, stat_ref, far_ref):
    n = q_ref.shape[0]
    k = jnp.concatenate([k_ref[...], kv_ref[:n]], 0)
    v = jnp.concatenate([v_ref[...], kv_ref[n:]], 0)
    s = nt(k, stack_heads(q_ref[...]))
    top = jnp.max(s, axis=0, keepdims=True)
    e = jnp.exp2((s - top) * (SCALE * LOG2E)).astype(BF16)
    p_ref[0] = e
    inverse = 1.0 / jnp.sum(e.astype(F32), axis=0, keepdims=True)
    stat_ref[0] = jnp.concatenate([top, inverse], 0)
    att_ref[...] = own_heads(mm(v.T, e) * inverse).astype(BF16)
    far_ref[...] = kv_ref[...]


def attend(q, k, v, kv, state, first, pairs, after):
    n, width = q.shape
    count = width // PAIR
    at = lambda *block: pl.BlockSpec((1, *block), lambda i: (first + i, 0, 0))
    return run(
        attend_kernel, "attend",
        [q, k, v, kv], [column(n, first)] * 3 + [column(2 * n, 0)],
        [
            ((width, n), BF16), ((2 * count, 2 * n, 2 * n), BF16),
            ((count, 2, 2 * n), F32), ((2 * n, width), BF16),
        ],
        [pl.BlockSpec((PAIR, n), lambda i: (first + i, 0)), at(2 * n, 2 * n), at(2, 2 * n), column(2 * n, first)],
        (pairs,), after, state, us=0.4 * pairs, vmem=BIG,
    )


def back_kernel(p_ref, stat_ref, q_ref, k_ref, v_ref, kv_ref, d_ref, dq_ref, dk_ref, dv_ref, out_ref):
    n = q_ref.shape[0]
    k = jnp.concatenate([k_ref[...], kv_ref[:n]], 0)
    v = jnp.concatenate([v_ref[...], kv_ref[n:]], 0)
    q = stack_heads(q_ref[...])
    d = spread_heads(d_ref[...])
    p = p_ref[0].astype(F32) * stat_ref[0, 1:]
    dp = mm(v, d)
    delta = jnp.sum(p * dp, axis=0, keepdims=True)
    ds = (p * (dp - delta)).astype(BF16)
    dv_ref[...] = nt(p[:n].astype(BF16), d)
    dk_ref[...] = mm(ds[:n], q)
    dq_ref[...] = (own_heads(mm(k.T, ds)) * SCALE).T.astype(BF16)
    out_ref[0] = jnp.concatenate([stat_ref[0], delta], 0)


def back(state, q, k, v, d, done, first, pairs, after):
    n, width = q.shape
    _, p, stat, kv = state
    at = lambda *block: pl.BlockSpec((1, *block), lambda i: (first + i, 0, 0))
    return run(
        back_kernel, "back",
        [p, stat, q, k, v, kv, d],
        [at(2 * n, 2 * n), at(2, 2 * n)]
        + [column(n, first)] * 3
        + [column(2 * n, first), pl.BlockSpec((PAIR, n), lambda i: (first + i, 0))],
        [((n, width), BF16)] + [((n, width), F32)] * 2 + [((width // PAIR, 3, 2 * n), F32)],
        [column(n, first)] * 3 + [at(3, 2 * n)],
        (pairs,), after, done, us=0.1 if first else 2 * pairs, vmem=BIG,
    )


def cross_kernel(q_ref, k_ref, v_ref, d_ref, stat_ref, dk_ref, dv_ref, gk_ref, gv_ref):
    q = stack_heads(q_ref[...])
    d = spread_heads(d_ref[...])
    top, inverse, delta = (stat_ref[0, i : i + 1] for i in range(3))
    e = jnp.exp2((nt(k_ref[...], q) - top) * (SCALE * LOG2E)).astype(BF16)
    p = e.astype(F32) * inverse
    ds = (p * (mm(v_ref[...], d) - delta)).astype(BF16)
    gv_ref[...] = (nt(p.astype(BF16), d) + dv_ref[...]).astype(BF16)
    gk_ref[...] = ((mm(ds, q) + dk_ref[...]) * SCALE).astype(BF16)


def cross(q, k, v, d, share, grads, first, pairs, after):
    n, width = q.shape
    dk, dv, stat = share
    return run(
        cross_kernel, "cross",
        [q, k, v, d, stat, dk, dv],
        [column(n, first)] * 3
        + [pl.BlockSpec((PAIR, n), lambda i: (first + i, 0)), pl.BlockSpec((1, 3, 2 * n), lambda i: (first + i, 0, 0))]
        + [column(n, first)] * 2,
        [((n, width), BF16)] * 2, [column(n, first)] * 2, (pairs,), after, grads, us=1.5 * pairs, vmem=BIG,
    )


def join(cam, mine, far, after):
    rows, half = mine.shape

    def kernel(cam_ref, mine_ref, far_ref, out_ref):
        for c, (left, right) in enumerate(((mine_ref, far_ref), (far_ref, mine_ref))):

            @pl.when(cam_ref[0] == c)
            def _():
                out_ref[:, :half] = left[...]
                out_ref[:, half:] = right[...]

    (out,), token = run(
        kernel, "join", [cam.reshape(1), mine, far], [SMEM, whole(mine), whole(far)],
        [((rows, 2 * half), BF16)], [whole((rows, 2 * half))], (1,), after, us=30,
    )
    return out, token


def copy(parts, after):
    rows, width = parts[0].shape
    count = len(parts)

    def kernel(*refs):
        for i, ref in enumerate(refs[:count]):
            refs[count][i * rows : (i + 1) * rows] = ref[...]

    (out,), token = run(
        kernel, "copy", parts, [whole(x) for x in parts],
        [((count * rows, width), BF16)], [whole((count * rows, width))], (1,), after, us=1,
    )
    return out, token


def project(w, own, other, after):
    rows, depth = w[0].shape
    n, parts, count = own.shape[0], len(w), sum(x.shape[0] for x in w) // rows

    def kernel(*refs):
        left = jnp.concatenate([r[...] for r in refs[:parts]], 0)
        for ref, out in zip(refs[parts : parts + 2], refs[parts + 2 :]):
            res = nt(left, ref[...]).astype(BF16)
            for j in range(count):
                out[j] = res[j * rows : (j + 1) * rows]

    tokens = pl.BlockSpec((PAIR, depth), lambda i: (i, 0))
    return run(
        kernel, "project", [*w, own, other],
        [whole(x) for x in w] + [tokens] * 2,
        [((count, rows, n), BF16)] * 2, [pl.BlockSpec((count, rows, PAIR), lambda i: (0, 0, i))] * 2,
        (n // PAIR,), after, us=count - 1.9,
    )


def weave(core, slots, mine, theirs, after):
    _, rows, n = mine[0].shape
    total = 2 * slots.shape[0]

    def kernel(slot_ref, core_ref, *refs):
        *refs, out = refs
        for side, which in enumerate((core_ref[0], 1 - core_ref[0])):
            place = 0
            for ref in refs[side * len(mine) : (side + 1) * len(mine)]:
                for j in range(ref.shape[0]):
                    out[2 * slot_ref[place] + which] = ref[j]
                    place += 1

    ins = [slots, core.reshape(1), *mine, *theirs]
    (out,), token = run(
        kernel, "weave", ins, [SMEM, SMEM] + [whole(x) for x in (*mine, *theirs)],
        [((total, rows, n), BF16)], [whole((total, rows, n))], (1,), after, us=2,
    )
    return out.reshape(total * rows, n), token


def outer(slots, a_own, a_other, own, other, groups, after):
    _, rows, n = a_own.shape
    depth = own.shape[1]
    count, tile = sum(groups), depth

    def kernel(slot_ref, *refs):
        mine, theirs, (own_ref, other_ref), outs = refs[:count], refs[count : 2 * count], refs[2 * count : 2 * count + 2], refs[2 * count + 2 :]
        left = [jnp.concatenate([r[0] for r in part], 0) for part in (mine, theirs)]
        right = jnp.concatenate([own_ref[...], other_ref[...]], 0)
        res = mm(jnp.concatenate(left, 1), right).astype(BF16)
        first = 0
        for out in outs:
            for j in range(out.shape[0]):
                out[j] = res[(first + j) * rows : (first + j + 1) * rows]
            first += out.shape[0]

    blocks = [pl.BlockSpec((1, rows, n), lambda i, slot, j=j: (slot[j], 0, 0)) for j in range(count)]
    return run(
        kernel, "outer", [a_own] * count + [a_other] * count + [own, other],
        blocks * 2 + [pl.BlockSpec((n, tile), lambda i, _: (0, i))] * 2,
        [((g, rows, depth), BF16) for g in groups],
        [pl.BlockSpec((g, rows, tile), lambda i, _: (0, 0, i)) for g in groups],
        (pl.cdiv(depth, tile),), after, slots=slots, us=6,
    )


def add_kernel(x_ref, y_ref, *outs):
    for j, out in enumerate(outs):
        out[...] = (x_ref[j].astype(F32) + y_ref[j].astype(F32)).astype(out.dtype)


def add(x, y, types, after):
    count, *block = x.shape
    return run(
        add_kernel, "add", [x, y], [whole(x), whole(y)], [(tuple(block), t) for t in types],
        [whole(tuple(block))] * count, (1,), after,
    )


def total_of(cam, parts, after):
    rows, width = parts[0].shape
    half = width // 2

    def kernel(cam_ref, *refs):
        *refs, mine, theirs = refs
        total = refs[0][...].astype(F32)
        for ref in refs[1:]:
            total += ref[...].astype(F32)
        left, right = total[:, :half], total[:, half:]
        for c, (x, y) in enumerate(((left, right), (right, left))):

            @pl.when(cam_ref[0] == c)
            def _():
                mine[...] = x
                theirs[...] = y.astype(BF16)

    return run(
        kernel, "total", [cam.reshape(1), *parts], [SMEM] + [whole(x) for x in parts],
        [((rows, half), F32), ((rows, half), BF16)], [whole((rows, half))] * 2, (1,), after,
    )


def last_sum(mine, theirs, scale, after):
    def kernel(x_ref, y_ref, out_ref):
        out_ref[...] = (x_ref[...] + y_ref[...].astype(F32)) * scale

    (out,), _ = run(
        kernel, "scale", [mine, theirs], [whole(mine)] * 2, [(mine.shape, F32)], [whole(mine)], (1,), after,
    )
    return out


def swap(x, axis, bit=1):
    size = lax.axis_size(axis)
    return lax.ppermute(x, axis, [(i, i ^ bit) for i in range(size)])


def shift(x, axis, step):
    size = lax.axis_size(axis)
    return lax.ppermute(x, axis, [(i, (i + step) % size) for i in range(size)])


def ordered(mine, theirs, flag, axis):
    return jnp.where(
        flag == 0,
        jnp.concatenate([mine, theirs], axis),
        jnp.concatenate([theirs, mine], axis),
    )


ORDER = (1, 3, 2)
LATE = (2, 1, 3, 0)


def body(queries, keys, values, d_out, w_out):
    shape = queries.shape
    width, model_width = shape[4], d_out.shape[4]
    n = shape[0] * shape[1] * shape[2] * shape[3]
    q, k, v = (x.reshape(n, width) for x in (queries, keys, values))
    flat = d_out.reshape(n, model_width)
    cams, bands, objs = (lax.axis_size(a) for a in ("cam", "band", "obj"))
    total = n * cams * bands * objs
    cam, band, obj = (lax.axis_index(a) for a in ("cam", "band", "obj"))
    core, line = obj % 2, obj // 2
    rows, half = w_out.shape
    blocked = bands == 4 and objs == 4
    sizes = CHUNKS if sum(CHUNKS) * PAIR == width else (1,) * (width // PAIR)
    chunks = [(sum(sizes[:i]), c) for i, c in enumerate(sizes)]

    scale = float(total) ** (-0.5)
    w_far = swap(w_out, "cam")
    sent, token = [], ()

    def send(i, after):
        packed, token = pack(k, v, *chunks[i], after)
        sent.append(swap(packed, "cam"))
        return (token,)

    def forward(i, state, after):
        state, token = attend(q, k, v, sent[i], state, *chunks[i], after)
        return state, (token,)

    def backward(i, dq, after):
        (dq, *share), token = back(state, q, k, v, d_att, dq, *parts[i], after)
        return (dq, *share), (token,)

    pairs = width // PAIR
    parts = [(sum(PARTS[:i]), c) for i, c in enumerate(PARTS)] if sum(PARTS) == pairs else [(0, pairs)]
    state, dq = (), ()
    if blocked and len(chunks) == len(parts) == 3:
        flat_other = swap(flat, "obj")
        into = [2 * band + line, 2 * band + 1 - line]
        into += [2 * ((band - s) % 4) + l for l in (line, 1 - line) for s in ORDER]
        into = jnp.stack(into).astype(jnp.int32)
        out_of = [4 * ((band + s) % 4) + 2 * l + core for l in (1 - line, line) for s in LATE]
        out_of = jnp.stack(out_of).astype(jnp.int32)

        after = send(0, ())
        w_cols, token = join(cam, w_out, w_far, after)
        held = [shift(w_cols, "band", s) for s in ORDER]
        y_own = swap(w_cols, "obj", 2)
        after = send(1, (token, flat_other))
        (mine_a, theirs_a), token = project([w_cols, y_own], flat, flat_other, after)
        theirs_a = swap(theirs_a, "obj")
        state, after = forward(0, state, (token,))
        x, token = copy(held[:2], after)
        y_near = swap(x, "obj", 2)
        after = send(2, (token,))
        state, after = forward(1, state, after)
        x, token = copy([q], after)
        q_far = swap(x, "cam")
        x, token = copy(held[2:], (token, y_near))
        y_far = swap(x, "obj", 2)
        state, after = forward(2, state, (token,))

        a_own = state[0].reshape(bands * objs, rows, n)
        a_other = swap(a_own, "obj")
        (*away, stay), token = outer(out_of, a_own, a_other, flat, flat_other, (1, 1, 2, 4), after)
        away = [swap(x, "obj", 2) for x in away]
        (mine_b, theirs_b), token = project([*held, y_near, y_far], flat, flat_other, (token,))
        theirs_b = swap(theirs_b, "obj")
        (x,), token = add(stay[:1], away[0], (BF16,), (token,))
        sums = [shift(x, "band", LATE[0])]
        d_att, token = weave(core, into, [mine_a, mine_b], [theirs_a, theirs_b], (token, q_far))
        d_far = swap(d_att, "cam")
        dq, after = backward(0, dq, (token,))
        (x,), token = add(stay[1:2], away[1], (BF16,), after)
        sums.append(shift(x, "band", LATE[1]))
        dq, after = backward(1, dq, (token,))
        (dq, *share), after = backward(2, dq, after)
        share[2] = swap(share[2], "cam")
        (x, base), token = add(stay[2:], away[2], (BF16, F32), (*after, sums[0]))
        sums.append(shift(x, "band", LATE[2]))
        grads, token = cross(q_far, k, v, d_far, share, (), 0, pairs // 2, (token, sums[1]))
        (mine, theirs), token = total_of(cam, [base, *sums], (token,))
        theirs = swap(theirs, "cam")
        grads, token = cross(q_far, k, v, d_far, share, grads, pairs // 2, pairs - pairs // 2, (token,))
    else:
        after, q_far = (), swap(q, "cam")
        for i in range(len(chunks)):
            after = send(i, after)
        for i in range(len(chunks)):
            state, after = forward(i, state, after)
        full = lax.all_gather(ordered(w_out, w_far, cam, 1), ("band", "obj"), axis=0, tiled=True)
        d_att = nt(full, flat).astype(BF16)
        d_far = swap(d_att, "cam")
        for i in range(len(parts)):
            dq, after = backward(i, dq, after)
        dq, *share = dq
        share[2] = swap(share[2], "cam")
        grads, token = cross(q_far, k, v, d_far, share, (), 0, pairs, after)
        sums = lax.psum_scatter(mm(state[0], flat), ("band", "obj"), scatter_dimension=0, tiled=True)
        mine = jnp.where(cam == 0, sums[:, :half], sums[:, half:])
        theirs = jnp.where(cam == 0, sums[:, half:], sums[:, :half])
        theirs = swap(theirs.astype(BF16), "cam")
    grad_wo = last_sum(mine, theirs, scale, (token,))
    return (dq.reshape(shape), grads[0].reshape(shape), grads[1].reshape(shape), grad_wo)


def solution(mesh):
    token = P("obj", "cam", "band", None, None)
    weight = P(("band", "obj"), "cam")
    return jax.shard_map(
        body,
        mesh=mesh,
        in_specs=(token, token, token, token, weight),
        out_specs=(token, token, token, weight),
        check_vma=False,
    )
```

```python
import jax
import jax.numpy as jnp
from jax import lax
from jax.experimental import pallas as pl
from jax.experimental.pallas import tpu as pltpu
from jax.sharding import PartitionSpec as P

BF16, F32 = jnp.bfloat16, jnp.float32
HEAD = 64
PAIR = 2 * HEAD
SCALE = HEAD**-0.5
LOG2E = 1.4426950408889634
NT = (((1,), (1,)), ((), ()))
ANY = pl.BlockSpec(memory_space=pl.ANY)
VMEM = pl.BlockSpec(memory_space=pltpu.VMEM)
SMEM = pl.BlockSpec(memory_space=pltpu.SMEM)
TOKEN = (8, 128)
BIG = 36
FLOPS_PER_US = 1150e6 * 0.5
CHUNKS = (3, 5, 2)
PARTS = (6, 3, 1)


def mm(a, b):
    return jnp.dot(a, b, preferred_element_type=F32)


def nt(a, b):
    return lax.dot_general(a, b, NT, preferred_element_type=F32)


def run(kernel, name, ins, in_specs, outs, out_specs, grid=(), after=(), alias=(), scratch=(), us=1, vmem=24, slots=None):
    hold = [*alias, *after]
    n_slots, n_in, n_hold, n_out = int(slots is not None), len(ins), len(hold), len(outs)

    def wrapped(*refs):
        last = n_slots + n_in + n_hold + n_out
        kernel(*refs[: n_slots + n_in], *refs[last - n_out : last], *refs[last + 1 :])
        refs[last][...] = jnp.zeros(TOKEN, F32)

    token_spec = pl.BlockSpec(TOKEN, lambda *_: (0, 0)) if grid else VMEM
    *results, token = pl.pallas_call(
        wrapped,
        grid_spec=pltpu.PrefetchScalarGridSpec(
            num_scalar_prefetch=n_slots,
            grid=grid,
            in_specs=[*in_specs, *[ANY] * n_hold],
            out_specs=[*out_specs, token_spec],
            scratch_shapes=list(scratch),
        ),
        out_shape=[*[jax.ShapeDtypeStruct(s, t) for s, t in outs], jax.ShapeDtypeStruct(TOKEN, F32)],
        input_output_aliases={n_slots + n_in + i: i for i in range(len(alias))},
        compiler_params=pltpu.CompilerParams(vmem_limit_bytes=vmem * 2**20),
        cost_estimate=pl.CostEstimate(flops=int(us * FLOPS_PER_US), transcendentals=0, bytes_accessed=0),
        name=name,
    )(*([] if slots is None else [slots]), *ins, *hold)
    return results, token


def whole(x):
    shape = x if isinstance(x, tuple) else x.shape
    return pl.BlockSpec(shape, lambda *_: (0,) * len(shape))


def stack_heads(x):
    lane = lax.broadcasted_iota(jnp.int32, x.shape, 1)
    zero = jnp.zeros_like(x)
    return jnp.concatenate([jnp.where(lane < HEAD, x, zero), jnp.where(lane < HEAD, zero, x)], 0)


def spread_heads(x):
    zero = jnp.zeros((HEAD, x.shape[1]), x.dtype)
    return jnp.concatenate(
        [jnp.concatenate([x[:HEAD], zero], 0), jnp.concatenate([zero, x[HEAD:]], 0)], 1
    )


def own_heads(x):
    n = x.shape[1] // 2
    return jnp.concatenate([x[:HEAD, :n], x[HEAD:, n:]], 0)


def column(n, first):
    return pl.BlockSpec((n, PAIR), lambda i: (0, first + i))


def pack_kernel(k_ref, v_ref, out_ref):
    n = k_ref.shape[0]
    out_ref[:n] = k_ref[...]
    out_ref[n:] = v_ref[...]


def pack(k, v, first, pairs, after):
    n = k.shape[0]
    (out,), token = run(
        pack_kernel, "pack", [k, v], [column(n, first)] * 2,
        [((2 * n, pairs * PAIR), BF16)], [column(2 * n, 0)], (pairs,), after, us=0.1,
    )
    return out, token


def attend_kernel(q_ref, k_ref, v_ref, kv_ref, att_ref, p_ref, stat_ref, far_ref):
    n = q_ref.shape[0]
    k = jnp.concatenate([k_ref[...], kv_ref[:n]], 0)
    v = jnp.concatenate([v_ref[...], kv_ref[n:]], 0)
    s = nt(k, stack_heads(q_ref[...]))
    top = jnp.max(s, axis=0, keepdims=True)
    e = jnp.exp2((s - top) * (SCALE * LOG2E)).astype(BF16)
    p_ref[0] = e
    inverse = 1.0 / jnp.sum(e.astype(F32), axis=0, keepdims=True)
    stat_ref[0] = jnp.concatenate([top, inverse], 0)
    att_ref[...] = own_heads(mm(v.T, e) * inverse).astype(BF16)
    far_ref[...] = kv_ref[...]


def attend(q, k, v, kv, state, first, pairs, after):
    n, width = q.shape
    count = width // PAIR
    at = lambda *block: pl.BlockSpec((1, *block), lambda i: (first + i, 0, 0))
    return run(
        attend_kernel, "attend",
        [q, k, v, kv], [column(n, first)] * 3 + [column(2 * n, 0)],
        [
            ((width, n), BF16), ((2 * count, 2 * n, 2 * n), BF16),
            ((count, 2, 2 * n), F32), ((2 * n, width), BF16),
        ],
        [pl.BlockSpec((PAIR, n), lambda i: (first + i, 0)), at(2 * n, 2 * n), at(2, 2 * n), column(2 * n, first)],
        (pairs,), after, state, us=0.4 * pairs, vmem=BIG,
    )


def back_kernel(p_ref, stat_ref, q_ref, k_ref, v_ref, kv_ref, d_ref, dq_ref, dk_ref, dv_ref, out_ref):
    n = q_ref.shape[0]
    k = jnp.concatenate([k_ref[...], kv_ref[:n]], 0)
    v = jnp.concatenate([v_ref[...], kv_ref[n:]], 0)
    q = stack_heads(q_ref[...])
    d = spread_heads(d_ref[...])
    p = p_ref[0].astype(F32) * stat_ref[0, 1:]
    dp = mm(v, d)
    delta = jnp.sum(p * dp, axis=0, keepdims=True)
    ds = (p * (dp - delta)).astype(BF16)
    dv_ref[...] = nt(p[:n].astype(BF16), d)
    dk_ref[...] = mm(ds[:n], q)
    dq_ref[...] = (own_heads(mm(k.T, ds)) * SCALE).T.astype(BF16)
    out_ref[0] = jnp.concatenate([stat_ref[0], delta], 0)


def back(state, q, k, v, d, done, first, pairs, after):
    n, width = q.shape
    _, p, stat, kv = state
    at = lambda *block: pl.BlockSpec((1, *block), lambda i: (first + i, 0, 0))
    return run(
        back_kernel, "back",
        [p, stat, q, k, v, kv, d],
        [at(2 * n, 2 * n), at(2, 2 * n)]
        + [column(n, first)] * 3
        + [column(2 * n, first), pl.BlockSpec((PAIR, n), lambda i: (first + i, 0))],
        [((n, width), BF16)] + [((n, width), F32)] * 2 + [((width // PAIR, 3, 2 * n), F32)],
        [column(n, first)] * 3 + [at(3, 2 * n)],
        (pairs,), after, done, us=0.1 if first else 2 * pairs, vmem=BIG,
    )


def cross_kernel(q_ref, k_ref, v_ref, d_ref, stat_ref, dk_ref, dv_ref, gk_ref, gv_ref):
    q = stack_heads(q_ref[...])
    d = spread_heads(d_ref[...])
    top, inverse, delta = (stat_ref[0, i : i + 1] for i in range(3))
    e = jnp.exp2((nt(k_ref[...], q) - top) * (SCALE * LOG2E)).astype(BF16)
    p = e.astype(F32) * inverse
    ds = (p * (mm(v_ref[...], d) - delta)).astype(BF16)
    gv_ref[...] = (nt(p.astype(BF16), d) + dv_ref[...]).astype(BF16)
    gk_ref[...] = ((mm(ds, q) + dk_ref[...]) * SCALE).astype(BF16)


def cross(q, k, v, d, share, grads, first, pairs, after):
    n, width = q.shape
    dk, dv, stat = share
    return run(
        cross_kernel, "cross",
        [q, k, v, d, stat, dk, dv],
        [column(n, first)] * 3
        + [pl.BlockSpec((PAIR, n), lambda i: (first + i, 0)), pl.BlockSpec((1, 3, 2 * n), lambda i: (first + i, 0, 0))]
        + [column(n, first)] * 2,
        [((n, width), BF16)] * 2, [column(n, first)] * 2, (pairs,), after, grads, us=1.5 * pairs, vmem=BIG,
    )


def join(cam, mine, far, after):
    rows, half = mine.shape

    def kernel(cam_ref, mine_ref, far_ref, out_ref):
        for c, (left, right) in enumerate(((mine_ref, far_ref), (far_ref, mine_ref))):

            @pl.when(cam_ref[0] == c)
            def _():
                out_ref[:, :half] = left[...]
                out_ref[:, half:] = right[...]

    (out,), token = run(
        kernel, "join", [cam.reshape(1), mine, far], [SMEM, whole(mine), whole(far)],
        [((rows, 2 * half), BF16)], [whole((rows, 2 * half))], (1,), after, us=30,
    )
    return out, token


def copy(parts, after):
    rows, width = parts[0].shape
    count = len(parts)

    def kernel(*refs):
        for i, ref in enumerate(refs[:count]):
            refs[count][i * rows : (i + 1) * rows] = ref[...]

    (out,), token = run(
        kernel, "copy", parts, [whole(x) for x in parts],
        [((count * rows, width), BF16)], [whole((count * rows, width))], (1,), after, us=1,
    )
    return out, token


def project(w, own, other, after):
    rows, depth = w[0].shape
    n, parts, count = own.shape[0], len(w), sum(x.shape[0] for x in w) // rows

    def kernel(*refs):
        left = jnp.concatenate([r[...] for r in refs[:parts]], 0)
        both = jnp.concatenate([r[...] for r in refs[parts : parts + 2]], 0)
        res = nt(left, both).astype(BF16)
        for i, out in enumerate(refs[parts + 2 :]):
            for j in range(count):
                out[j] = res[j * rows : (j + 1) * rows, i * PAIR : (i + 1) * PAIR]

    tokens = pl.BlockSpec((PAIR, depth), lambda i: (i, 0))
    return run(
        kernel, "project", [*w, own, other],
        [whole(x) for x in w] + [tokens] * 2,
        [((count, rows, n), BF16)] * 2, [pl.BlockSpec((count, rows, PAIR), lambda i: (0, 0, i))] * 2,
        (n // PAIR,), after, us=count - 1.9,
    )


def weave(core, slots, mine, theirs, after):
    _, rows, n = mine[0].shape
    total = 2 * slots.shape[0]

    def kernel(slot_ref, core_ref, *refs):
        *refs, out = refs
        for side, which in enumerate((core_ref[0], 1 - core_ref[0])):
            place = 0
            for ref in refs[side * len(mine) : (side + 1) * len(mine)]:
                for j in range(ref.shape[0]):
                    out[2 * slot_ref[place] + which] = ref[j]
                    place += 1

    ins = [slots, core.reshape(1), *mine, *theirs]
    (out,), token = run(
        kernel, "weave", ins, [SMEM, SMEM] + [whole(x) for x in (*mine, *theirs)],
        [((total, rows, n), BF16)], [whole((total, rows, n))], (1,), after, us=2,
    )
    return out.reshape(total * rows, n), token


def outer(slots, a_own, a_other, own, other, groups, after):
    _, rows, n = a_own.shape
    depth = own.shape[1]
    count, tile = sum(groups), depth

    def kernel(slot_ref, *refs):
        mine, theirs, (own_ref, other_ref), outs = refs[:count], refs[count : 2 * count], refs[2 * count : 2 * count + 2], refs[2 * count + 2 :]
        left = [jnp.concatenate([r[0] for r in part], 0) for part in (mine, theirs)]
        right = jnp.concatenate([own_ref[...], other_ref[...]], 0)
        res = mm(jnp.concatenate(left, 1), right).astype(BF16)
        first = 0
        for out in outs:
            for j in range(out.shape[0]):
                out[j] = res[(first + j) * rows : (first + j + 1) * rows]
            first += out.shape[0]

    blocks = [pl.BlockSpec((1, rows, n), lambda i, slot, j=j: (slot[j], 0, 0)) for j in range(count)]
    return run(
        kernel, "outer", [a_own] * count + [a_other] * count + [own, other],
        blocks * 2 + [pl.BlockSpec((n, tile), lambda i, _: (0, i))] * 2,
        [((g, rows, depth), BF16) for g in groups],
        [pl.BlockSpec((g, rows, tile), lambda i, _: (0, 0, i)) for g in groups],
        (pl.cdiv(depth, tile),), after, slots=slots, us=6,
    )


def add_kernel(x_ref, y_ref, *outs):
    for j, out in enumerate(outs):
        out[...] = (x_ref[j].astype(F32) + y_ref[j].astype(F32)).astype(out.dtype)


def add(x, y, types, after):
    count, *block = x.shape
    return run(
        add_kernel, "add", [x, y], [whole(x), whole(y)], [(tuple(block), t) for t in types],
        [whole(tuple(block))] * count, (1,), after,
    )


def total_of(cam, parts, after):
    rows, width = parts[0].shape
    half = width // 2

    def kernel(cam_ref, *refs):
        *refs, mine, theirs = refs
        total = refs[0][...].astype(F32)
        for ref in refs[1:]:
            total += ref[...].astype(F32)
        left, right = total[:, :half], total[:, half:]
        for c, (x, y) in enumerate(((left, right), (right, left))):

            @pl.when(cam_ref[0] == c)
            def _():
                mine[...] = x
                theirs[...] = y.astype(BF16)

    return run(
        kernel, "total", [cam.reshape(1), *parts], [SMEM] + [whole(x) for x in parts],
        [((rows, half), F32), ((rows, half), BF16)], [whole((rows, half))] * 2, (1,), after,
    )


def last_sum(mine, theirs, scale, after):
    def kernel(x_ref, y_ref, out_ref):
        out_ref[...] = (x_ref[...] + y_ref[...].astype(F32)) * scale

    (out,), _ = run(
        kernel, "scale", [mine, theirs], [whole(mine)] * 2, [(mine.shape, F32)], [whole(mine)], (1,), after,
    )
    return out


def swap(x, axis, bit=1):
    size = lax.axis_size(axis)
    return lax.ppermute(x, axis, [(i, i ^ bit) for i in range(size)])


def shift(x, axis, step):
    size = lax.axis_size(axis)
    return lax.ppermute(x, axis, [(i, (i + step) % size) for i in range(size)])


def ordered(mine, theirs, flag, axis):
    return jnp.where(
        flag == 0,
        jnp.concatenate([mine, theirs], axis),
        jnp.concatenate([theirs, mine], axis),
    )


ORDER = (1, 3, 2)
LATE = (2, 1, 3, 0)


def body(queries, keys, values, d_out, w_out):
    shape = queries.shape
    width, model_width = shape[4], d_out.shape[4]
    n = shape[0] * shape[1] * shape[2] * shape[3]
    q, k, v = (x.reshape(n, width) for x in (queries, keys, values))
    flat = d_out.reshape(n, model_width)
    cams, bands, objs = (lax.axis_size(a) for a in ("cam", "band", "obj"))
    total = n * cams * bands * objs
    cam, band, obj = (lax.axis_index(a) for a in ("cam", "band", "obj"))
    core, line = obj % 2, obj // 2
    rows, half = w_out.shape
    blocked = bands == 4 and objs == 4
    sizes = CHUNKS if sum(CHUNKS) * PAIR == width else (1,) * (width // PAIR)
    chunks = [(sum(sizes[:i]), c) for i, c in enumerate(sizes)]

    scale = float(total) ** (-0.5)
    w_far = swap(w_out, "cam")
    sent, token = [], ()

    def send(i, after):
        packed, token = pack(k, v, *chunks[i], after)
        sent.append(swap(packed, "cam"))
        return (token,)

    def forward(i, state, after):
        state, token = attend(q, k, v, sent[i], state, *chunks[i], after)
        return state, (token,)

    def backward(i, dq, after):
        (dq, *share), token = back(state, q, k, v, d_att, dq, *parts[i], after)
        return (dq, *share), (token,)

    pairs = width // PAIR
    parts = [(sum(PARTS[:i]), c) for i, c in enumerate(PARTS)] if sum(PARTS) == pairs else [(0, pairs)]
    state, dq = (), ()
    if blocked and len(chunks) == len(parts) == 3:
        flat_other = swap(flat, "obj")
        into = [2 * band + line, 2 * band + 1 - line]
        into += [2 * ((band - s) % 4) + l for l in (line, 1 - line) for s in ORDER]
        into = jnp.stack(into).astype(jnp.int32)
        out_of = [4 * ((band + s) % 4) + 2 * l + core for l in (1 - line, line) for s in LATE]
        out_of = jnp.stack(out_of).astype(jnp.int32)

        after = send(0, ())
        w_cols, token = join(cam, w_out, w_far, after)
        held = [shift(w_cols, "band", s) for s in ORDER]
        y_own = swap(w_cols, "obj", 2)
        after = send(1, (token, flat_other))
        (mine_a, theirs_a), token = project([w_cols, y_own], flat, flat_other, after)
        theirs_a = swap(theirs_a, "obj")
        state, after = forward(0, state, (token,))
        x, token = copy(held[:2], after)
        y_near = swap(x, "obj", 2)
        after = send(2, (token,))
        state, after = forward(1, state, after)
        x, token = copy([q], after)
        q_far = swap(x, "cam")
        x, token = copy(held[2:], (token, y_near))
        y_far = swap(x, "obj", 2)
        state, after = forward(2, state, (token,))

        a_own = state[0].reshape(bands * objs, rows, n)
        a_other = swap(a_own, "obj")
        (*away, stay), token = outer(out_of, a_own, a_other, flat, flat_other, (1, 1, 2, 4), after)
        away = [swap(x, "obj", 2) for x in away]
        (mine_b, theirs_b), token = project([*held, y_near, y_far], flat, flat_other, (token,))
        theirs_b = swap(theirs_b, "obj")
        (x,), token = add(stay[:1], away[0], (BF16,), (token,))
        sums = [shift(x, "band", LATE[0])]
        d_att, token = weave(core, into, [mine_a, mine_b], [theirs_a, theirs_b], (token, q_far))
        d_far = swap(d_att, "cam")
        dq, after = backward(0, dq, (token,))
        (x,), token = add(stay[1:2], away[1], (BF16,), after)
        sums.append(shift(x, "band", LATE[1]))
        dq, after = backward(1, dq, (token,))
        (dq, *share), after = backward(2, dq, after)
        share[2] = swap(share[2], "cam")
        (x, base), token = add(stay[2:], away[2], (BF16, F32), (*after, sums[0]))
        sums.append(shift(x, "band", LATE[2]))
        grads, token = cross(q_far, k, v, d_far, share, (), 0, pairs // 2, (token, sums[1]))
        (mine, theirs), token = total_of(cam, [base, *sums], (token,))
        theirs = swap(theirs, "cam")
        grads, token = cross(q_far, k, v, d_far, share, grads, pairs // 2, pairs - pairs // 2, (token,))
    else:
        after, q_far = (), swap(q, "cam")
        for i in range(len(chunks)):
            after = send(i, after)
        for i in range(len(chunks)):
            state, after = forward(i, state, after)
        full = lax.all_gather(ordered(w_out, w_far, cam, 1), ("band", "obj"), axis=0, tiled=True)
        d_att = nt(full, flat).astype(BF16)
        d_far = swap(d_att, "cam")
        for i in range(len(parts)):
            dq, after = backward(i, dq, after)
        dq, *share = dq
        share[2] = swap(share[2], "cam")
        grads, token = cross(q_far, k, v, d_far, share, (), 0, pairs, after)
        sums = lax.psum_scatter(mm(state[0], flat), ("band", "obj"), scatter_dimension=0, tiled=True)
        mine = jnp.where(cam == 0, sums[:, :half], sums[:, half:])
        theirs = jnp.where(cam == 0, sums[:, half:], sums[:, :half])
        theirs = swap(theirs.astype(BF16), "cam")
    grad_wo = last_sum(mine, theirs, scale, (token,))
    return (dq.reshape(shape), grads[0].reshape(shape), grads[1].reshape(shape), grad_wo)


def solution(mesh):
    token = P("obj", "cam", "band", None, None)
    weight = P(("band", "obj"), "cam")
    return jax.shard_map(
        body,
        mesh=mesh,
        in_specs=(token, token, token, token, weight),
        out_specs=(token, token, token, weight),
        check_vma=False,
    )
```
